768 devices in a mesh: graph: 24 (over z, core), dp: 32 (over x, y).
Axes of the slice: x: 4, y: 8, z: 12, core: 2. Of those that a mesh axis runs over, the one named last changes fastest.
Arguments:
- node_features: bfloat16 [32, 49, 64, 3072], P('dp', None, None, 'graph'), may hold values from -6 to 6
- cotangent: bfloat16 [32, 49, 64, 3072], P('dp', None, None, 'graph'), may hold values from -6 to 6
- wigner: bfloat16 [128, 29, 49], replicated, as said below
- w_zero: bfloat16 [448, 448], replicated, may hold values from -0.25 to 0.25
- w_one: bfloat16 [2, 384, 384], replicated, may hold values from -0.21875 to 0.21875
- w_two: bfloat16 [2, 320, 320], replicated, may hold values from -0.25 to 0.25
- edge_source: int32 [32, 3072], P('dp', 'graph'), may hold values from 0 to 127
- edge_target: int32 [32, 3072], P('dp', 'graph'), may hold values from 0 to 127
- edge_bin: int32 [32, 3072], P('dp', 'graph'), may hold values from 0 to 127
- edge_scale: float32 [32, 3072], P('dp', 'graph'), may hold values from 0.25 to 1
- send_atoms: int32 [32, 48, 32], P('dp', 'graph'), may hold values from 0 to 127
- send_bins: int32 [32, 48, 32], P('dp', 'graph'), may hold values from 0 to 127, as said below
- recv_targets: int32 [32, 48, 32], P('dp', 'graph'), may hold values from 0 to 127
- recv_bins: int32 [32, 48, 32], P('dp', 'graph'), may hold values from 0 to 127
- recv_scale: float32 [32, 48, 32], P('dp', 'graph'), may hold values from 0.25 to 1
Outputs:
- updated: bfloat16 [32, 49, 64, 3072], P('dp', None, None, 'graph')
- feature_grad: float32 [32, 49, 64, 3072], P('dp', None, None, 'graph')
- grad_zero: float32 [448, 448], replicated
- grad_one: float32 [2, 384, 384], replicated
- grad_two: float32 [2, 320, 320], replicated
The draws below stay inside these ranges and needn't reach their ends.
Inputs may be any that keep to these rules, and one draw needn't show every extreme that they name: `wigner`: nonzero only between rows of the same degree l; entries independent. `send_bins`: block 0 of graph index s equals recv_bins slot 1 of index s - 1, block 1 equals slot 0 of index s + 1, cyclically.
All inputs are finite; a program needn't handle non-finite values.
Results may differ from the reference program's by a relative error of at most 0.0056.
Values may be sent and summed in bfloat16 or wider, within the bound.
No kernel may reach another device: no remote copies, remote signals or barrier semaphores. Data moves between devices by JAX's collectives and lax.ppermute only.
A program may use at most 128 MiB of HBM per device.

```python
import math
import jax
import jax.numpy as jnp
import numpy as np
from jax import lax

COEF = 49
TRUNC = 29
CH = 64
NBINS = 128
A_DEV = 128
E_DEV = 128
CAP = 32
SLABS = 32
ATOMS = 3072
EDGES = 3072
HALO_ROWS = 48
N_GRAPH = 24


def degree_table():
    row_degrees = list(range(7)) + list(range(1, 7)) + list(range(1, 7)) + list(range(2, 7)) + list(range(2, 7))
    col_degrees = [math.isqrt(index) for index in range(COEF)]
    rows = np.array(row_degrees)[:, None]
    cols = np.array(col_degrees)[None, :]
    return np.where(rows == cols, 1.0 / np.sqrt(2.0 * rows + 1.0), 0.0).astype(np.float32)


def draw_wigner(key, part):
    key = jax.random.fold_in(key, 11)
    masked = jnp.asarray(degree_table())
    values = jax.random.normal(key, (NBINS, TRUNC, COEF), jnp.float32)
    return (values * masked[None]).astype(jnp.bfloat16)


def shared_bins(key):
    return jax.random.randint(key, (SLABS, HALO_ROWS, CAP), 0, NBINS, dtype=jnp.int32)


def draw_recv_bins(key, part):
    return shared_bins(key)


def draw_send_bins(key, part):
    base = shared_bins(key).reshape(SLABS, HALO_ROWS // 2, 2, CAP)
    to_lower = jnp.roll(base[:, :, 1], 1, axis=1)
    to_upper = jnp.roll(base[:, :, 0], -1, axis=1)
    return jnp.stack([to_lower, to_upper], axis=2).reshape(SLABS, HALO_ROWS, CAP)


def touch_ends(drawn, rng, least, high):
    shape = drawn.shape
    spot = [jax.random.randint(jax.random.fold_in(rng, axis), (), 0, shape[axis]) for axis in range(len(shape))]
    drawn = drawn.at[tuple(spot)].set(least)
    longest = shape.index(max(shape))
    spot[longest] = (spot[longest] + 1) % shape[longest]
    return drawn.at[tuple(spot)].set(high)


def block_levels(rng, dims, cuts, least, largest):
    gain, own = 1.0, jax.random.fold_in(rng, 6)
    for dim, blocks in cuts:
        steps = jnp.exp(jax.random.uniform(jax.random.fold_in(own, dim), (blocks,), jnp.float32, least / len(cuts), largest / len(cuts)))
        gain = gain * jnp.repeat(steps, dims[dim] // blocks).reshape([-1 if axis == dim else 1 for axis in range(len(dims))])
    return gain


def centred(own_key, extent, deviation, reach, shards=(), kind=jnp.bfloat16):
    level = block_levels(own_key, extent, shards, -0.22, 0.18) if shards else 1.0
    values = jax.random.normal(own_key, extent, jnp.float32) * deviation * level
    return jnp.minimum(jnp.maximum(values, -reach), reach).astype(kind)


def setup_inputs(seed: int = 0) -> dict:
    key_of = jax.random.split(jax.random.key(seed), 16)
    return {
        "node_features": centred(key_of[0], (SLABS, COEF, CH, ATOMS), 1.0, 6.0, ((0, 32), (3, 24))),
        "cotangent": centred(key_of[1], (SLABS, COEF, CH, ATOMS), 1.0, 6.0, ((0, 32), (3, 24))),
        "wigner": draw_wigner(jax.random.fold_in(key_of[15], 71), 0),
        "w_zero": centred(key_of[3], (7 * CH, 7 * CH), (7 * CH) ** -0.5, 0.25),
        "w_one": centred(key_of[4], (2, 6 * CH, 6 * CH), (12 * CH) ** -0.5, 0.21875),
        "w_two": centred(key_of[5], (2, 5 * CH, 5 * CH), (10 * CH) ** -0.5, 0.25),
        "edge_source": touch_ends(jax.random.randint(key_of[6], (SLABS, EDGES), 0, A_DEV), jax.random.fold_in(key_of[6], 1), 0, A_DEV - 1).astype(jnp.int32),
        "edge_target": touch_ends(jax.random.randint(key_of[7], (SLABS, EDGES), 0, A_DEV), jax.random.fold_in(key_of[7], 1), 0, A_DEV - 1).astype(jnp.int32),
        "edge_bin": touch_ends(jax.random.randint(key_of[8], (SLABS, EDGES), 0, NBINS), jax.random.fold_in(key_of[8], 1), 0, NBINS - 1).astype(jnp.int32),
        "edge_scale": jnp.clip(jnp.exp(math.log(1.0) - 1.3862944 * jax.random.uniform(key_of[9], (SLABS, EDGES), jnp.float32) ** block_levels(key_of[9], (SLABS, EDGES), ((0, 32), (1, 24)), -0.2, 0.2)), 0.25, 1.0),
        "send_atoms": touch_ends(jax.random.randint(key_of[10], (SLABS, HALO_ROWS, CAP), 0, A_DEV), jax.random.fold_in(key_of[10], 1), 0, A_DEV - 1).astype(jnp.int32),
        "send_bins": draw_send_bins(jax.random.fold_in(key_of[15], 71), 0),
        "recv_targets": touch_ends(jax.random.randint(key_of[12], (SLABS, HALO_ROWS, CAP), 0, A_DEV), jax.random.fold_in(key_of[12], 1), 0, A_DEV - 1).astype(jnp.int32),
        "recv_bins": draw_recv_bins(jax.random.fold_in(key_of[15], 71), 0),
        "recv_scale": jnp.clip(jnp.exp(math.log(1.0) - 1.3862944 * jax.random.uniform(key_of[14], (SLABS, HALO_ROWS, CAP), jnp.float32) ** block_levels(key_of[14], (SLABS, HALO_ROWS, CAP), ((0, 32), (1, 24)), -0.2, 0.2)), 0.25, 1.0),
    }


def product(left, right):
    return jnp.dot(left, right, preferred_element_type=jnp.float32)


def product_t(left, right):
    return lax.dot_general(left, right, (((0,), (0,)), ((), ())), preferred_element_type=jnp.float32)


def outer_sum(left, right):
    return lax.dot_general(left, right, (((1,), (1,)), ((), ())), preferred_element_type=jnp.float32)


def split_orders(values):
    channels = values.shape[1]
    count = values.shape[2]
    return [values[0:7].reshape(7 * channels, count), values[7:13].reshape(6 * channels, count),
            values[13:19].reshape(6 * channels, count), values[19:24].reshape(5 * channels, count),
            values[24:29].reshape(5 * channels, count)]


def join_orders(pieces, channels, count):
    return jnp.concatenate([piece.reshape(-1, channels, count) for piece in pieces], axis=0)


def convolve(rotated, w_zero, w_one, w_two):
    parts = split_orders(rotated)
    outputs = [product(w_zero, parts[0]),
               product(w_one[0], parts[1]) - product(w_one[1], parts[2]),
               product(w_one[1], parts[1]) + product(w_one[0], parts[2]),
               product(w_two[0], parts[3]) - product(w_two[1], parts[4]),
               product(w_two[1], parts[3]) + product(w_two[0], parts[4])]
    return join_orders(outputs, rotated.shape[1], rotated.shape[2])


def convolve_back(conv_grad, rotated, w_zero, w_one, w_two):
    grads = split_orders(conv_grad)
    parts = split_orders(rotated)
    inputs = [product_t(w_zero, grads[0]),
              product_t(w_one[0], grads[1]) + product_t(w_one[1], grads[2]),
              product_t(w_one[0], grads[2]) - product_t(w_one[1], grads[1]),
              product_t(w_two[0], grads[3]) + product_t(w_two[1], grads[4]),
              product_t(w_two[0], grads[4]) - product_t(w_two[1], grads[3])]
    grad_zero = outer_sum(grads[0], parts[0])
    grad_one = jnp.stack([outer_sum(grads[1], parts[1]) + outer_sum(grads[2], parts[2]),
                          outer_sum(grads[2], parts[1]) - outer_sum(grads[1], parts[2])])
    grad_two = jnp.stack([outer_sum(grads[3], parts[3]) + outer_sum(grads[4], parts[4]),
                          outer_sum(grads[4], parts[3]) - outer_sum(grads[3], parts[4])])
    return join_orders(inputs, rotated.shape[1], rotated.shape[2]), (grad_zero, grad_one, grad_two)


def reference(node_features, cotangent, wigner, w_zero, w_one, w_two, edge_source, edge_target, edge_bin,
              edge_scale, send_atoms, send_bins, recv_targets, recv_bins, recv_scale):
    graphs = N_GRAPH
    owner = jnp.arange(EDGES, dtype=jnp.int32) // E_DEV
    local_rank = jnp.arange(graphs, dtype=jnp.int32)[:, None]
    sender = (local_rank + jnp.array([[-1, 1]], dtype=jnp.int32)) % graphs
    block_of = jnp.zeros((graphs, 2), jnp.int32) + jnp.array([[1, 0]], dtype=jnp.int32)

    def per_slab(pieces):
        (node_slab, cot_slab, int_src, int_tgt, int_bin, int_scale, out_atoms, out_bins, in_tgt, in_bins,
         in_scale) = pieces
        out_atoms = out_atoms.reshape(graphs, 2, CAP)
        out_bins = out_bins.reshape(graphs, 2, CAP)
        halo_src = (sender[:, :, None] * A_DEV + out_atoms[sender, block_of]).reshape(-1)
        halo_bin = out_bins[sender, block_of].reshape(-1)
        halo_tgt = (local_rank[:, :, None] * A_DEV + in_tgt.reshape(graphs, 2, CAP)).reshape(-1)
        sources = jnp.concatenate([owner * A_DEV + int_src, halo_src]).astype(jnp.int32)
        targets = jnp.concatenate([owner * A_DEV + int_tgt, halo_tgt]).astype(jnp.int32)
        bins_in = jnp.concatenate([int_bin, halo_bin]).astype(jnp.int32)
        bins_out = jnp.concatenate([int_bin, in_bins.reshape(-1)]).astype(jnp.int32)
        scales = jnp.concatenate([int_scale, in_scale.reshape(-1)])
        frames_in = wigner[bins_in].astype(jnp.float32)
        frames_out = wigner[bins_out].astype(jnp.float32)
        gathered = jnp.take(node_slab, sources, axis=2).astype(jnp.float32)
        rotated = jnp.einsum('erk,kce->rce', frames_in, gathered).astype(jnp.bfloat16)
        conv_out = convolve(rotated, w_zero, w_one, w_two)
        gating = jax.nn.sigmoid(conv_out[0])
        factor = gating * scales[None, :]
        message = conv_out * factor[None]
        node_part = jnp.einsum('erk,rce->kce', frames_out, message).astype(jnp.bfloat16)
        summed = jax.ops.segment_sum(jnp.moveaxis(node_part.astype(jnp.float32), 2, 0), targets, num_segments=ATOMS)
        updated = (node_slab.astype(jnp.float32) + 0.5 * jnp.moveaxis(summed, 0, 2)).astype(jnp.bfloat16)
        node_grad = 0.5 * jnp.take(cot_slab, targets, axis=2).astype(jnp.float32)
        message_grad = jnp.einsum('erk,kce->rce', frames_out, node_grad)
        factor_grad = jnp.sum(message_grad * conv_out, axis=0)
        conv_grad = message_grad * factor[None]
        conv_grad = conv_grad.at[0].add(factor_grad * scales[None, :] * gating * (1.0 - gating))
        conv_grad = conv_grad.astype(jnp.bfloat16)
        input_grad, weight_grads = convolve_back(conv_grad, rotated, w_zero, w_one, w_two)
        input_grad = input_grad.astype(jnp.bfloat16)
        source_grad = jnp.einsum('erk,rce->kce', frames_in, input_grad.astype(jnp.float32)).astype(jnp.bfloat16)
        scattered = jax.ops.segment_sum(jnp.moveaxis(source_grad.astype(jnp.float32), 2, 0), sources,
                                        num_segments=ATOMS)
        feature_grad = cot_slab.astype(jnp.float32) + jnp.moveaxis(scattered, 0, 2)
        return updated, feature_grad, weight_grads[0], weight_grads[1], weight_grads[2]

    results = lax.map(per_slab, (node_features, cotangent, edge_source, edge_target, edge_bin, edge_scale,
                                 send_atoms, send_bins, recv_targets, recv_bins, recv_scale))
    return (results[0], results[1], jnp.sum(results[2], axis=0) / SLABS, jnp.sum(results[3], axis=0) / SLABS,
            jnp.sum(results[4], axis=0) / SLABS)
```

```python
import functools

import jax
import jax.numpy as jnp
from jax import lax
from jax.experimental import pallas as pl
from jax.experimental.pallas import tpu as pltpu
from jax.sharding import PartitionSpec as P

COEF, TRUNC, CH, LANES = 49, 29, 64, 128
CAP, GROUPS, SUB = 32, 4, 16
ROWS = TRUNC * CH
PAD_ROWS = 32
ZERO, PLUS1, MINUS1, PLUS2, MINUS2 = (0, 448), (448, 832), (832, 1216), (1216, 1536), (1536, 1856)
VMEM = 56 * 1024 * 1024
f32, bf16 = jnp.float32, jnp.bfloat16


def degree_rows(degree):
    rows = [degree]
    if degree >= 1:
        rows = rows + [6 + degree, 12 + degree]
    if degree >= 2:
        rows = rows + [17 + degree, 22 + degree]
    return rows


def dot(left, right):
    return jnp.dot(left, right, preferred_element_type=f32)


def dot_nt(left, right):
    return lax.dot_general(left, right, (((1,), (1,)), ((), ())), preferred_element_type=f32)


def dot_tn(left, right):
    return lax.dot_general(left, right, (((0,), (0,)), ((), ())), preferred_element_type=f32)


def iota(shape, axis):
    return lax.broadcasted_iota(jnp.int32, shape, axis)


def one_hot(index, value=1.0):
    lanes = index.shape[1]
    return jnp.where(iota((LANES, lanes), 0) == index, value, 0.0).astype(f32).astype(bf16)


def one_hot_rows(index_row, value=1.0):
    return one_hot(index_row, value)


def load_frames(frames, padded, wigner, bins):
    padded[:, 0:TRUNC, :] = wigner[...]
    lanes = bins.shape[1]
    found = dot(padded[...].reshape(COEF * PAD_ROWS, LANES), one_hot(bins))
    frames[...] = found.reshape(COEF, PAD_ROWS, lanes)


def rotate_into(frames, values, found, chunk):
    channels = values.shape[1]

    def step(index, carry):
        part = pl.ds(pl.multiple_of(index * chunk, chunk), chunk)
        for degree in range(7):
            rows = degree_rows(degree)
            total = {}
            for k in range(degree * degree, (degree + 1) * (degree + 1)):
                value = values[k, part, :].astype(f32)
                for row in rows:
                    term = frames[k, row : row + 1, :] * value
                    total[row] = term if row not in total else total[row] + term
            for row in rows:
                found[row, part, :] = total[row].astype(found.dtype)
        return carry

    lax.fori_loop(0, channels // chunk, step, 0)


def rotate_back(frames, values, found, chunk):
    channels = values.shape[1]

    def step(index, carry):
        part = pl.ds(pl.multiple_of(index * chunk, chunk), chunk)
        for degree in range(7):
            rows = degree_rows(degree)
            held = {row: values[row, part, :].astype(f32) for row in rows}
            for k in range(degree * degree, (degree + 1) * (degree + 1)):
                total = None
                for row in rows:
                    term = frames[k, row : row + 1, :] * held[row]
                    total = term if total is None else total + term
                found[k, part, :] = total.astype(found.dtype)
        return carry

    lax.fori_loop(0, channels // chunk, step, 0)


def flat(value):
    return value.reshape(value.shape[0] * value.shape[1], value.shape[2])


def halo_row(pair, fill):
    rest = jnp.full((1, LANES - 2 * CAP), fill, pair.dtype)
    return jnp.concatenate([pair[0:1, :], pair[1:2, :], rest], axis=1)


def packed_row(pair):
    pieces = [pair[slot : slot + 1, :] for slot in range(2) for _ in range(GROUPS)]
    return jnp.concatenate(pieces, axis=1)


def rim_kernel(node, wigner, atoms, bins, to_lower, to_upper, frames, padded, gathered, rotated):
    load_frames(frames, padded, wigner, packed_row(bins[...]))
    row = packed_row(atoms[...])
    wide = 2 * LANES
    group = (iota((GROUPS * LANES, wide), 1) & (LANES - 1)) >> 5
    entry = iota((GROUPS * LANES, wide), 0)
    table = jnp.where(entry == row + group * LANES, 1.0, 0.0).astype(f32).astype(bf16)
    left = jnp.concatenate(
        [flat(node[:, g * SUB : (g + 1) * SUB, :]) for g in range(GROUPS)], axis=1
    )
    gathered[...] = dot(left, table).reshape(COEF, SUB, wide)
    rotate_into(frames, gathered, rotated, SUB)
    to_lower[...] = rotated[:, :, 0:LANES]
    to_upper[...] = rotated[:, :, LANES:wide]


def conv_forward(rotated, conv, w_zero, w_one, w_two):
    def rows(span):
        return flat(rotated[span[0] // CH : span[1] // CH])

    def put(span, value):
        conv[span[0] // CH : span[1] // CH] = value.reshape(-1, CH, LANES)

    put(ZERO, dot(w_zero[...], rows(ZERO)))
    put(PLUS1, dot(w_one[0], rows(PLUS1)) - dot(w_one[1], rows(MINUS1)))
    put(MINUS1, dot(w_one[1], rows(PLUS1)) + dot(w_one[0], rows(MINUS1)))
    put(PLUS2, dot(w_two[0], rows(PLUS2)) - dot(w_two[1], rows(MINUS2)))
    put(MINUS2, dot(w_two[1], rows(PLUS2)) + dot(w_two[0], rows(MINUS2)))


def edge_work(rotated, frames, cot, targets, scale, weights, conv, message_grad, values, conv_grad, message):
    conv_forward(rotated, conv, *weights)
    values[...] = dot(flat(cot[...]), one_hot(targets, 0.5)).reshape(COEF, CH, LANES)
    rotate_into(frames, values, message_grad, 32)
    gating = jax.nn.sigmoid(conv[0])
    factor = gating * scale
    factor_grad = message_grad[0] * conv[0]
    for row in range(1, TRUNC):
        factor_grad = factor_grad + message_grad[row] * conv[row]
    extra = factor_grad * scale * gating * (1.0 - gating)
    for row in range(TRUNC):
        grad = message_grad[row] * factor
        if row == 0:
            grad = grad + extra
        conv_grad[row] = grad.astype(bf16)
        message[row] = conv[row] * factor


def inner_kernel(
    node, cot, wigner, w_zero, w_one, w_two, sources, targets, bins, scale,
    rotated, conv_grad, message,
    frames, padded, values, conv, message_grad,
):
    load_frames(frames, padded, wigner, bins[...])
    values[...] = dot(flat(node[...]), one_hot(sources[...])).reshape(COEF, CH, LANES)
    rotate_into(frames, values, rotated, 32)
    edge_work(rotated, frames, cot, targets[...], scale[...], (w_zero, w_one, w_two),
              conv, message_grad, values, conv_grad, message)


def spread_table():
    shape = (2 * LANES, GROUPS * LANES)
    lane, column = iota(shape, 0), iota(shape, 1)
    slot, where = lane >> 7, lane & (LANES - 1)
    group, inside = column >> 7, column & (LANES - 1)
    same = (where >> 5 == group) & (inside == slot * CAP + (where & (CAP - 1)))
    return jnp.where(same, 1.0, 0.0).astype(f32).astype(bf16)


def pack_grads(packed, zero, one, two):
    at = 0
    for value in [zero] + one + two:
        height, width = value.shape
        for first in range(0, width - LANES + 1, LANES):
            packed[at : at + height, :] = value[:, first : first + LANES].astype(bf16)
            at += height
        if width % LANES:
            first, half = width - width % LANES, height // 2
            piece = value[:, first:width]
            packed[at : at + half, :] = jnp.concatenate([piece[0:half], piece[half:]], axis=1).astype(bf16)
            at += half
    if at < packed.shape[0]:
        packed[at:, :] = jnp.zeros((packed.shape[0] - at, LANES), bf16)


def halo_kernel(
    core, from_lower, from_upper, cot, wigner, w_zero, w_one, w_two, targets, bins, scale, inner_rotated, inner_grad,
    conv_grad, message, keep, send,
    frames, padded, rotated, values, conv, message_grad, packed,
):
    load_frames(frames, padded, wigner, halo_row(bins[...], -1))
    left = jnp.concatenate([flat(from_lower[...]), flat(from_upper[...])], axis=1)
    spread = dot(left, spread_table()).astype(bf16)
    for g in range(GROUPS):
        rotated[:, g * SUB : (g + 1) * SUB, :] = spread[:, g * LANES : (g + 1) * LANES].reshape(TRUNC, SUB, LANES)
    edge_work(rotated, frames, cot, halo_row(targets[...], -1), halo_row(scale[...], 0.0), (w_zero, w_one, w_two),
              conv, message_grad, values, conv_grad, message)

    def grads(span):
        part = slice(span[0] // CH, span[1] // CH)
        return jnp.concatenate([flat(inner_grad[part]), flat(conv_grad[part])], axis=1)

    def inputs(span):
        part = slice(span[0] // CH, span[1] // CH)
        return jnp.concatenate([flat(inner_rotated[part]), flat(rotated[part])], axis=1)

    zero = dot_nt(grads(ZERO), inputs(ZERO))
    pairs = []
    for plus, minus in ((PLUS1, MINUS1), (PLUS2, MINUS2)):
        pairs.append([
            dot_nt(grads(plus), inputs(plus)) + dot_nt(grads(minus), inputs(minus)),
            dot_nt(grads(minus), inputs(plus)) - dot_nt(grads(plus), inputs(minus)),
        ])
    pack_grads(packed, zero, pairs[0], pairs[1])
    half = packed.shape[0] // 2
    keep[...] = packed[pl.ds(pl.multiple_of(core[0] * half, SUB), half), :]
    send[...] = packed[pl.ds(pl.multiple_of((1 - core[0]) * half, SUB), half), :]


def input_kernel(
    inner_grad, halo_grad, wigner, w_zero, w_one, w_two, bins, sources, cot,
    to_lower, to_upper, feature_grad,
    frames, padded, joint, source_grad,
):
    def grads(span):
        part = slice(span[0] // CH, span[1] // CH)
        return jnp.concatenate([flat(inner_grad[part]), flat(halo_grad[part])], axis=1)

    def put(span, value):
        joint[span[0] // CH : span[1] // CH] = value.astype(bf16).reshape(-1, CH, 2 * LANES)

    put(ZERO, dot_tn(w_zero[...], grads(ZERO)))
    for weights, plus, minus in ((w_one, PLUS1, MINUS1), (w_two, PLUS2, MINUS2)):
        put(plus, dot_tn(weights[0], grads(plus)) + dot_tn(weights[1], grads(minus)))
        put(minus, dot_tn(weights[0], grads(minus)) - dot_tn(weights[1], grads(plus)))
    left = jnp.concatenate(
        [flat(joint[:, g * SUB : (g + 1) * SUB, LANES : 2 * LANES]) for g in range(GROUPS)], axis=1
    )
    shape = (GROUPS * LANES, 2 * LANES)
    column, lane = iota(shape, 0), iota(shape, 1)
    slot, where = lane >> 7, lane & (LANES - 1)
    group, inside = column >> 7, column & (LANES - 1)
    same = (where >> 5 == group) & (inside == slot * CAP + (where & (CAP - 1)))
    gathered = dot(left, jnp.where(same, 1.0, 0.0).astype(f32).astype(bf16)).astype(bf16)
    to_lower[...] = gathered[:, 0:LANES].reshape(TRUNC, SUB, LANES)
    to_upper[...] = gathered[:, LANES : 2 * LANES].reshape(TRUNC, SUB, LANES)
    load_frames(frames, padded, wigner, bins[...])
    rotate_back(frames, joint.at[:, :, 0:LANES], source_grad, 32)
    scattered = dot_nt(flat(source_grad[...]), one_hot(sources[...])).reshape(COEF, CH, LANES)
    feature_grad[...] = cot[...].astype(f32) + scattered


def update_kernel(
    node, wigner, inner_message, halo_message, inner_bins, inner_targets, halo_bins, halo_targets,
    updated, frames, padded, inner_part, halo_part,
):
    load_frames(frames, padded, wigner, inner_bins[...])
    rotate_back(frames, inner_message, inner_part, 32)
    load_frames(frames, padded, wigner, halo_row(halo_bins[...], -1))
    rotate_back(frames, halo_message, halo_part, 32)
    left = jnp.concatenate([flat(inner_part[...]), flat(halo_part[...])], axis=1)
    table = jnp.concatenate(
        [one_hot(inner_targets[...], 0.5), one_hot(halo_row(halo_targets[...], -1), 0.5)], axis=1
    )
    summed = dot_nt(left, table).reshape(COEF, CH, LANES)
    updated[...] = (node[...].astype(f32) + summed).astype(bf16)


def back_kernel(
    back_zero, back_one, wigner, bins, atoms, partial, feature_grad,
    frames, padded, joint, source_grad,
):
    load_frames(frames, padded, wigner, packed_row(bins[...]))
    joint[:, :, 0:LANES] = back_zero[...]
    joint[:, :, LANES : 2 * LANES] = back_one[...]
    rotate_back(frames, joint, source_grad, SUB)
    row = packed_row(atoms[...])
    wide = 2 * LANES
    group = (iota((LANES, wide), 1) & (LANES - 1)) >> 5
    entry = iota((LANES, wide), 0)
    values = flat(source_grad[...])
    for g in range(GROUPS):
        table = jnp.where((entry == row) & (group == g), 1.0, 0.0).astype(f32).astype(bf16)
        scattered = dot_nt(values, table).reshape(COEF, SUB, LANES)
        part = slice(g * SUB, (g + 1) * SUB)
        feature_grad[:, part, :] = partial[:, part, :] + scattered


def unpack_kernel(replicas, core, mine, other, zero, one, two, packed):
    half = packed.shape[0] // 2
    packed[pl.ds(pl.multiple_of(core[0] * half, SUB), half), :] = flat(mine[...])
    packed[pl.ds(pl.multiple_of((1 - core[0]) * half, SUB), half), :] = flat(other[...])
    at = 0
    refs = [zero] + [one.at[0], one.at[1]] + [two.at[0], two.at[1]]
    for ref in refs:
        height, width = ref.shape
        for first in range(0, width - LANES + 1, LANES):
            ref[:, first : first + LANES] = packed[at : at + height, :].astype(f32) * (1.0 / replicas)
            at += height
        if width % LANES:
            first, half = width - width % LANES, height // 2
            value = packed[at : at + half, :].astype(f32) * (1.0 / replicas)
            ref[0:half, first:width] = value[:, 0 : width - first]
            ref[half:height, first:width] = value[:, width - first :]
            at += half


def call(kernel, outs, scratch, operands, flops, name, scalars=0):
    whole = pl.BlockSpec(memory_space=pltpu.VMEM)
    scalar = pl.BlockSpec(memory_space=pltpu.SMEM)
    moved = sum(v.size * v.dtype.itemsize for v in list(operands) + list(outs))
    return pl.pallas_call(
        kernel,
        out_shape=tuple(outs),
        in_specs=[scalar] * scalars + [whole] * (len(operands) - scalars),
        out_specs=tuple([whole] * len(outs)),
        scratch_shapes=scratch,
        compiler_params=pltpu.CompilerParams(vmem_limit_bytes=VMEM),
        cost_estimate=pl.CostEstimate(flops=flops, bytes_accessed=moved, transcendentals=0),
        name=name,
    )(*operands)


def arr(shape, dtype):
    return jax.ShapeDtypeStruct(shape, dtype)


def scr(shape, dtype):
    return pltpu.VMEM(shape, dtype)


def swap_cores(value):
    return lax.ppermute(value, "core", [(0, 1), (1, 0)])


def add_up(values):
    return jnp.sum(values.astype(f32), axis=0).astype(bf16)


def to_all(value, axes):
    copies = jnp.broadcast_to(value[None], (lax.axis_size(axes),) + value.shape)
    return lax.all_to_all(copies, axes, 0, 0)


def reduce_all(keep, send):
    plane = ("x", "y")
    pieces = lax.axis_size(plane)
    joint = (keep.astype(f32) + swap_cores(send).astype(f32)).astype(bf16)
    piece = add_up(lax.all_to_all(joint.reshape(pieces, -1, LANES), plane, 0, 0))
    piece = add_up(to_all(piece, "z"))
    mine = to_all(piece, plane)
    return mine, swap_cores(mine)


def from_behind(value, axis, steps):
    count = lax.axis_size(axis)
    return lax.ppermute(value, axis, [(source, (source + steps) % count) for source in range(count)])


PACKED = 5632


def body(
    node_features, cotangent, wigner, w_zero, w_one, w_two, edge_source, edge_target, edge_bin, edge_scale,
    send_atoms, send_bins, recv_targets, recv_bins, recv_scale,
):
    node, cot = node_features[0], cotangent[0]
    table = jnp.transpose(wigner, (2, 1, 0))
    graph = ("z", "core")
    out_atoms, out_bins = send_atoms[0], send_bins[0]
    in_targets, in_bins, in_scale = recv_targets[0], recv_bins[0], recv_scale[0]
    weights = [w_zero, w_one, w_two]
    packed_shape = arr((TRUNC, SUB, LANES), bf16)
    edges16, edges32 = arr((TRUNC, CH, LANES), bf16), arr((TRUNC, CH, LANES), f32)
    frames1, frames2 = scr((COEF, PAD_ROWS, LANES), f32), scr((COEF, PAD_ROWS, 2 * LANES), f32)
    padded = scr((COEF, PAD_ROWS, LANES), bf16)
    atoms32, rows32 = scr((COEF, CH, LANES), f32), scr((TRUNC, CH, LANES), f32)

    to_lower, to_upper = call(
        rim_kernel, [packed_shape] * 2,
        [frames2, padded, scr((COEF, SUB, 2 * LANES), f32), scr((TRUNC, SUB, 2 * LANES), bf16)],
        [node, table, out_atoms, out_bins], 10**9, "rim",
    )
    from_lower = from_behind(to_upper, graph, 1)
    from_upper = from_behind(to_lower, graph, -1)
    inner_rotated, inner_grad, inner_message = call(
        inner_kernel, [edges16, edges16, edges32],
        [frames1, padded, atoms32, rows32, rows32],
        [node, cot, table] + weights + [edge_source, edge_target, edge_bin, edge_scale], 10**10, "inner",
    )
    core = lax.axis_index("core").reshape(1)
    half = arr((PACKED // 2, LANES), bf16)
    halo_grad, halo_message, keep, send = call(
        halo_kernel, [edges16, edges32, half, half],
        [frames1, padded, scr((TRUNC, CH, LANES), bf16), atoms32, rows32, rows32, scr((PACKED, LANES), bf16)],
        [core, from_lower, from_upper, cot, table] + weights + [in_targets, in_bins, in_scale, inner_rotated, inner_grad],
        10**10, "halo", scalars=1,
    )
    mine, other = reduce_all(keep, send)
    back_lower, back_upper, partial = call(
        input_kernel, [packed_shape, packed_shape, arr((COEF, CH, LANES), f32)],
        [frames1, padded, scr((TRUNC, CH, 2 * LANES), bf16), scr((COEF, CH, LANES), bf16)],
        [inner_grad, halo_grad, table] + weights + [edge_bin, edge_source, cot], 10**10, "inputs",
    )
    back_zero = from_behind(back_upper, graph, 1)
    back_one = from_behind(back_lower, graph, -1)
    (updated,) = call(
        update_kernel, [arr((COEF, CH, LANES), bf16)],
        [frames1, padded, scr((COEF, CH, LANES), bf16), scr((COEF, CH, LANES), bf16)],
        [node, table, inner_message, halo_message, edge_bin, edge_target, in_bins, in_targets], 10**10, "update",
    )
    (feature_grad,) = call(
        back_kernel, [arr((COEF, CH, LANES), f32)],
        [frames2, padded, scr((TRUNC, SUB, 2 * LANES), bf16), scr((COEF, SUB, 2 * LANES), bf16)],
        [back_zero, back_one, table, out_bins, out_atoms, partial], 10**10, "back",
    )
    grad_zero, grad_one, grad_two = call(
        functools.partial(unpack_kernel, lax.axis_size(("x", "y"))), [arr(w_zero.shape, f32), arr(w_one.shape, f32), arr(w_two.shape, f32)],
        [scr((PACKED, LANES), bf16)], [core, mine, other], 0, "unpack", scalars=1,
    )
    return updated[None], feature_grad[None], grad_zero, grad_one, grad_two


def solution(mesh):
    cores, rows, columns = 2, 4, 8
    graph, replicas = mesh.shape["graph"], mesh.shape["dp"]
    if (graph, replicas) != (24, 32):
        cores, rows, columns = SMALL
    fine = jax.sharding.Mesh(mesh.devices.reshape(graph // cores, cores, rows, columns), ("z", "core", "x", "y"))
    dp, along = ("x", "y"), ("z", "core")
    nodes, edges = P(dp, None, None, along), P(dp, along)
    in_specs = (nodes, nodes) + (P(),) * 4 + (edges,) * 4 + (P(dp, along, None),) * 5
    return jax.shard_map(
        body, mesh=fine, in_specs=in_specs, out_specs=(nodes, nodes, P(), P(), P()), check_vma=False
    )
```

```python
import functools

import jax
import jax.numpy as jnp
from jax import lax
from jax.experimental import pallas as pl
from jax.experimental.pallas import tpu as pltpu
from jax.sharding import PartitionSpec as P

COEF, TRUNC, CH, LANES = 49, 29, 64, 128
CAP, GROUPS, SUB = 32, 4, 16
WIDE = 2 * LANES
PAD_ROWS = 32
ZERO, PLUS1, MINUS1, PLUS2, MINUS2 = (0, 448), (448, 832), (832, 1216), (1216, 1536), (1536, 1856)
VMEM = 24 * 1024 * 1024
f32, bf16 = jnp.float32, jnp.bfloat16


def degree_rows(degree):
    rows = [degree]
    if degree >= 1:
        rows = rows + [6 + degree, 12 + degree]
    if degree >= 2:
        rows = rows + [17 + degree, 22 + degree]
    return rows


def dot(left, right):
    return jnp.dot(left, right, preferred_element_type=f32)


def dot_nt(left, right):
    return lax.dot_general(left, right, (((1,), (1,)), ((), ())), preferred_element_type=f32)


def dot_tn(left, right):
    return lax.dot_general(left, right, (((0,), (0,)), ((), ())), preferred_element_type=f32)


def iota(shape, axis):
    return lax.broadcasted_iota(jnp.int32, shape, axis)


def one_hot(index, value=1.0):
    lanes = index.shape[1]
    return jnp.where(iota((LANES, lanes), 0) == index, value, 0.0).astype(f32).astype(bf16)


def load_frames(frames, padded, wigner, bins):
    padded[:, 0:TRUNC, :] = wigner[...]
    lanes = bins.shape[1]
    found = dot(padded[...].reshape(COEF * PAD_ROWS, LANES), one_hot(bins))
    frames[...] = found.reshape(COEF, PAD_ROWS, lanes)


def rotate_into(frames, values, found, chunk):
    channels = values.shape[1]

    def step(index, carry):
        part = pl.ds(pl.multiple_of(index * chunk, chunk), chunk)
        for degree in range(7):
            rows = degree_rows(degree)
            total = {}
            for k in range(degree * degree, (degree + 1) * (degree + 1)):
                value = values[k, part, :].astype(f32)
                for row in rows:
                    term = frames[k, row : row + 1, :] * value
                    total[row] = term if row not in total else total[row] + term
            for row in rows:
                found[row, part, :] = total[row].astype(found.dtype)
        return carry

    lax.fori_loop(0, channels // chunk, step, 0)


def rotate_back(frames, values, found, chunk):
    channels = values.shape[1]

    def step(index, carry):
        part = pl.ds(pl.multiple_of(index * chunk, chunk), chunk)
        for degree in range(7):
            rows = degree_rows(degree)
            held = {row: values[row, part, :].astype(f32) for row in rows}
            for k in range(degree * degree, (degree + 1) * (degree + 1)):
                total = None
                for row in rows:
                    term = frames[k, row : row + 1, :] * held[row]
                    total = term if total is None else total + term
                found[k, part, :] = total.astype(found.dtype)
        return carry

    lax.fori_loop(0, channels // chunk, step, 0)


def flat(value):
    return value.reshape(value.shape[0] * value.shape[1], value.shape[2])


def halo_row(pair, fill):
    rest = jnp.full((1, LANES - 2 * CAP), fill, pair.dtype)
    return jnp.concatenate([pair[0:1, :], pair[1:2, :], rest], axis=1)


def packed_row(pair):
    pieces = [pair[slot : slot + 1, :] for slot in range(2) for _ in range(GROUPS)]
    return jnp.concatenate(pieces, axis=1)


def rim_kernel(
    node_far, wigner_far, atoms_far, bins_far, to_lower, to_upper,
    frames, padded, gathered, rotated, node, wigner, atoms, bins, sems,
):
    pairs = [(wigner_far, wigner), (bins_far, bins), (atoms_far, atoms), (node_far, node)]
    copies = [pltpu.make_async_copy(far, near, sems.at[index]) for index, (far, near) in enumerate(pairs)]
    for copy in copies:
        copy.start()
    for copy in copies[0:3]:
        copy.wait()
    load_frames(frames, padded, wigner, packed_row(bins[...]))
    copies[3].wait()
    row = packed_row(atoms[...])
    wide = 2 * LANES
    group = (iota((GROUPS * LANES, wide), 1) & (LANES - 1)) >> 5
    entry = iota((GROUPS * LANES, wide), 0)
    table = jnp.where(entry == row + group * LANES, 1.0, 0.0).astype(f32).astype(bf16)
    left = jnp.concatenate(
        [flat(node[:, g * SUB : (g + 1) * SUB, :]) for g in range(GROUPS)], axis=1
    )
    gathered[...] = dot(left, table).reshape(COEF, SUB, wide)
    rotate_into(frames, gathered, rotated, SUB)
    to_lower[...] = rotated[:, :, 0:LANES]
    to_upper[...] = rotated[:, :, LANES:wide]


def pre_kernel(node, wigner, sources, bins, rotated_far, frames, padded, values, rotated, sem):
    load_frames(frames, padded, wigner, bins[...])
    values[...] = dot(flat(node[...]), one_hot(sources[...])).reshape(COEF, CH, LANES)
    rotate_into(frames, values, rotated, 32)
    copy = pltpu.make_async_copy(rotated, rotated_far, sem)
    copy.start()
    copy.wait()


def rows_of(values, first, last):
    return flat(values[first[0] // CH : last[1] // CH])


def conv_forward(rotated, conv, w_zero, w_one, w_two):
    def put(span, value):
        conv[span[0] // CH : span[1] // CH] = value.reshape(-1, CH, WIDE)

    put(ZERO, dot(w_zero[...], rows_of(rotated, ZERO, ZERO)))
    both = rows_of(rotated, PLUS1, MINUS1)
    put(PLUS1, dot(jnp.concatenate([w_one[0], -w_one[1]], axis=1), both))
    put(MINUS1, dot(jnp.concatenate([w_one[1], w_one[0]], axis=1), both))
    plus, minus = rows_of(rotated, PLUS2, PLUS2), rows_of(rotated, MINUS2, MINUS2)
    put(PLUS2, dot(w_two[0], plus) - dot(w_two[1], minus))
    put(MINUS2, dot(w_two[1], plus) + dot(w_two[0], minus))


def spread_table():
    shape = (2 * LANES, GROUPS * LANES)
    lane, column = iota(shape, 0), iota(shape, 1)
    slot, where = lane >> 7, lane & (LANES - 1)
    group, inside = column >> 7, column & (LANES - 1)
    same = (where >> 5 == group) & (inside == slot * CAP + (where & (CAP - 1)))
    return jnp.where(same, 1.0, 0.0).astype(f32).astype(bf16)


def pack_grads(packed, values):
    at = 0
    for value in values:
        height, width = value.shape
        for first in range(0, width - LANES + 1, LANES):
            packed[at : at + height, :] = value[:, first : first + LANES].astype(bf16)
            at += height
        if width % LANES:
            first, half = width - width % LANES, height // 2
            piece = value[:, first:width]
            packed[at : at + half, :] = jnp.concatenate([piece[0:half], piece[half:]], axis=1).astype(bf16)
            at += half
    packed[at:, :] = jnp.zeros((packed.shape[0] - at, LANES), bf16)


def conv_kernel(
    core, from_lower, from_upper, cot, wigner, targets, bins, halo_targets, halo_bins, w_zero, w_one, w_two,
    scale, halo_scale, inner_rotated,
    conv_grad_far, message, keep, send,
    rotated, conv, packed, message_grad, conv_grad, frames, padded, values, sems,
):
    get_rotated = pltpu.make_async_copy(inner_rotated, rotated.at[:, :, 0:LANES], sems.at[0])
    get_rotated.start()
    joint_bins = jnp.concatenate([bins[...], halo_row(halo_bins[...], -1)], axis=1)
    joint_targets = jnp.concatenate([targets[...], halo_row(halo_targets[...], -1)], axis=1)
    load_frames(frames, padded, wigner, joint_bins)
    values[...] = dot(flat(cot[...]), one_hot(joint_targets, 0.5)).reshape(COEF, CH, WIDE)
    rotate_into(frames, values, message_grad, 16)
    left = jnp.concatenate([flat(from_lower[...]), flat(from_upper[...])], axis=1)
    spread = dot(left, spread_table()).astype(bf16)
    for g in range(GROUPS):
        rotated[:, g * SUB : (g + 1) * SUB, LANES:WIDE] = spread[:, g * LANES : (g + 1) * LANES].reshape(
            TRUNC, SUB, LANES
        )
    get_rotated.wait()
    conv_forward(rotated, conv, w_zero, w_one, w_two)
    weight = jnp.concatenate([scale[...], halo_row(halo_scale[...], 0.0)], axis=1)
    gating = jax.nn.sigmoid(conv[0])
    factor = gating * weight
    factor_grad = message_grad[0] * conv[0]
    for row in range(1, TRUNC):
        value = conv[row]
        grad = message_grad[row]
        factor_grad = factor_grad + grad * value
        conv_grad[row] = (grad * factor).astype(bf16)
        message[row] = value * factor
    conv_grad[0] = (message_grad[0] * factor + factor_grad * weight * gating * (1.0 - gating)).astype(bf16)
    message[0] = conv[0] * factor
    put = pltpu.make_async_copy(conv_grad, conv_grad_far, sems.at[1])
    put.start()

    zero = dot_nt(rows_of(conv_grad, ZERO, ZERO), rows_of(rotated, ZERO, ZERO))
    pairs = []
    for plus, minus in ((PLUS1, MINUS1), (PLUS2, MINUS2)):
        g_plus, g_minus = rows_of(conv_grad, plus, plus), rows_of(conv_grad, minus, minus)
        inputs = jnp.concatenate([rows_of(rotated, plus, plus), rows_of(rotated, minus, minus)], axis=1)
        pairs.append([
            dot_nt(jnp.concatenate([g_plus, g_minus], axis=1), inputs),
            dot_nt(jnp.concatenate([g_minus, -g_plus], axis=1), inputs),
        ])
    one, two = pairs
    pack_grads(packed.at[0], [zero, one[0]])
    pack_grads(packed.at[1], [one[1]] + two)
    keep[...] = packed[core[0]]
    send[...] = packed[1 - core[0]]
    put.wait()


def input_kernel(conv_grad, w_zero, w_one, w_two, after, to_lower, to_upper, inner, joint):
    def put(span, value):
        joint[span[0] // CH : span[1] // CH] = value.astype(bf16).reshape(-1, CH, WIDE)

    put(ZERO, dot_tn(w_zero[...], rows_of(conv_grad, ZERO, ZERO)))
    for weights, plus, minus in ((w_one, PLUS1, MINUS1), (w_two, PLUS2, MINUS2)):
        both = flat(weights[...])
        put(plus, dot_tn(both, rows_of(conv_grad, plus, minus)))
        crossed = jnp.concatenate([rows_of(conv_grad, minus, minus), -rows_of(conv_grad, plus, plus)], axis=0)
        put(minus, dot_tn(both, crossed))
    left = jnp.concatenate(
        [flat(joint[:, g * SUB : (g + 1) * SUB, LANES:WIDE]) for g in range(GROUPS)], axis=1
    )
    shape = (GROUPS * LANES, WIDE)
    column, lane = iota(shape, 0), iota(shape, 1)
    slot, where = lane >> 7, lane & (LANES - 1)
    group, inside = column >> 7, column & (LANES - 1)
    same = (where >> 5 == group) & (inside == slot * CAP + (where & (CAP - 1)))
    gathered = dot(left, jnp.where(same, 1.0, 0.0).astype(f32).astype(bf16)).astype(bf16)
    to_lower[...] = gathered[:, 0:LANES].reshape(TRUNC, SUB, LANES)
    to_upper[...] = gathered[:, LANES:WIDE].reshape(TRUNC, SUB, LANES)
    inner[...] = joint[:, :, 0:LANES]


def update_kernel(
    node, wigner, message, bins, targets, halo_bins, halo_targets, after,
    updated, token, frames, padded, part,
):
    joint_bins = jnp.concatenate([bins[...], halo_row(halo_bins[...], -1)], axis=1)
    joint_targets = jnp.concatenate([targets[...], halo_row(halo_targets[...], -1)], axis=1)
    load_frames(frames, padded, wigner, joint_bins)
    rotate_back(frames, message, part, 16)
    summed = dot_nt(flat(part[...]), one_hot(joint_targets, 0.5)).reshape(COEF, CH, LANES)
    updated[...] = (node[...].astype(f32) + summed).astype(bf16)
    token[...] = jnp.zeros(token.shape, token.dtype)


def back_kernel(
    back_zero, back_one, inner, wigner, rim_bins, atoms, bins, sources, cot, after, feature_grad, token,
    frames, inner_frames, padded, joint, rim_grad, inner_grad,
):
    load_frames(inner_frames, padded, wigner, bins[...])
    rotate_back(inner_frames, inner, inner_grad, 32)
    load_frames(frames, padded, wigner, packed_row(rim_bins[...]))
    joint[:, :, 0:LANES] = back_zero[...]
    joint[:, :, LANES:WIDE] = back_one[...]
    rotate_back(frames, joint, rim_grad, SUB)
    row = packed_row(atoms[...])
    group = (iota((LANES, WIDE), 1) & (LANES - 1)) >> 5
    entry = iota((LANES, WIDE), 0)
    values = flat(rim_grad[...])
    inner_table = one_hot(sources[...])
    for g in range(GROUPS):
        part = slice(g * SUB, (g + 1) * SUB)
        table = jnp.where((entry == row) & (group == g), 1.0, 0.0).astype(f32).astype(bf16)
        scattered = dot_nt(values, table) + dot_nt(flat(inner_grad[:, part, :]), inner_table)
        feature_grad[:, part, :] = cot[:, part, :].astype(f32) + scattered.reshape(COEF, SUB, LANES)
    token[...] = jnp.zeros(token.shape, token.dtype)


def add_kernel(pieces, after, total):
    found = pieces[0].astype(f32)
    for index in range(1, pieces.shape[0]):
        found = found + pieces[index].astype(f32)
    found = found.astype(bf16)
    if total.ndim == 2:
        total[...] = found
    else:
        for index in range(total.shape[0]):
            total[index] = found


def join_kernel(keep, other, joint):
    joint[...] = (keep[...].astype(f32) + other[...].astype(f32)).astype(bf16)


def unpack_kernel(replicas, swapped, which, packed, *refs):
    (zero, one, two), (zero_v, one_v, two_v), sems = refs[-7:-4], refs[-4:-1], refs[-1]

    def write(pairs):
        at = 0
        copies = []
        for index, (ref, out) in enumerate(pairs):
            height, width = ref.shape
            for first in range(0, width - LANES + 1, LANES):
                ref[:, first : first + LANES] = packed[at : at + height, :].astype(f32) * (1.0 / replicas)
                at += height
            if width % LANES:
                first, part = width - width % LANES, height // 2
                value = packed[at : at + part, :].astype(f32) * (1.0 / replicas)
                ref[0:part, first:width] = value[:, 0 : width - first]
                ref[part:height, first:width] = value[:, width - first :]
                at += part
            copy = pltpu.make_async_copy(ref, out, sems.at[index])
            copy.start()
            copies.append(copy)
        for copy in copies:
            copy.wait()

    half = 1 - which[0] if swapped else which[0]

    @pl.when(half == 0)
    def first():
        write([(zero_v, zero), (one_v.at[0], one.at[0])])

    @pl.when(half == 1)
    def second():
        write([(one_v.at[1], one.at[1]), (two_v.at[0], two.at[0]), (two_v.at[1], two.at[1])])


def call(kernel, outs, scratch, operands, flops, name, scalars=0, far=0, hbm=0, far_outs=0, aliases=None):
    whole = pl.BlockSpec(memory_space=pltpu.VMEM)
    scalar = pl.BlockSpec(memory_space=pltpu.SMEM)
    away = pl.BlockSpec(memory_space=pl.ANY)
    main = pl.BlockSpec(memory_space=pltpu.HBM)
    moved = sum(v.size * v.dtype.itemsize for v in list(operands) + list(outs))
    operands = list(operands)
    for index in range(len(operands) - hbm, len(operands)):
        operands[index] = pltpu.with_memory_space_constraint(operands[index], pltpu.HBM)
    outs = [pltpu.HBM(v.shape, v.dtype) if index < far_outs else v for index, v in enumerate(outs)]
    near = len(operands) - scalars - far - hbm
    return pl.pallas_call(
        kernel,
        out_shape=tuple(outs),
        in_specs=[scalar] * scalars + [whole] * near + [away] * far + [main] * hbm,
        out_specs=tuple([main] * far_outs + [whole] * (len(outs) - far_outs)),
        scratch_shapes=scratch,
        input_output_aliases=aliases or {},
        compiler_params=pltpu.CompilerParams(vmem_limit_bytes=VMEM),
        cost_estimate=pl.CostEstimate(flops=flops, bytes_accessed=moved, transcendentals=0),
        name=name,
    )(*operands)


def arr(shape, dtype):
    return jax.ShapeDtypeStruct(shape, dtype)


def scr(shape, dtype):
    return pltpu.VMEM(shape, dtype)


def from_behind(value, axis, steps):
    count = lax.axis_size(axis)
    return lax.ppermute(value, axis, [(source, (source + steps) % count) for source in range(count)])


def swap_cores(value):
    return lax.ppermute(value, "core", [(0, 1), (1, 0)])


def to_all(copies, axes):
    return lax.all_to_all(copies, axes, 0, 0)


PACKED = 5632
SPLIT = (2, 4, 8)
PLANE = ("x", "y")


def body(
    node_features, cotangent, wigner, w_zero, w_one, w_two, edge_source, edge_target, edge_bin, edge_scale,
    send_atoms, send_bins, recv_targets, recv_bins, recv_scale,
):
    node, cot = node_features[0], cotangent[0]
    table = jnp.transpose(wigner, (2, 1, 0))
    graph = ("z", "core")
    out_atoms, out_bins = send_atoms[0], send_bins[0]
    in_targets, in_bins, in_scale = recv_targets[0], recv_bins[0], recv_scale[0]
    weights = [w_zero, w_one, w_two]
    packed_shape = arr((TRUNC, SUB, LANES), bf16)
    edges16, edges32 = arr((TRUNC, CH, WIDE), bf16), arr((TRUNC, CH, WIDE), f32)
    frames1, frames2 = scr((COEF, PAD_ROWS, LANES), f32), scr((COEF, PAD_ROWS, WIDE), f32)
    padded = scr((COEF, PAD_ROWS, LANES), bf16)
    mark = arr((8, LANES), f32)

    to_lower, to_upper = call(
        rim_kernel, [packed_shape] * 2,
        [frames2, padded, scr((COEF, SUB, WIDE), f32), scr((TRUNC, SUB, WIDE), bf16),
         scr(node.shape, bf16), scr(table.shape, bf16), scr(out_atoms.shape, jnp.int32),
         scr(out_bins.shape, jnp.int32), pltpu.SemaphoreType.DMA((4,))],
        [node, table, out_atoms, out_bins], 10**9, "rim", hbm=4,
    )
    from_lower = from_behind(to_upper, graph, 1)
    from_upper = from_behind(to_lower, graph, -1)
    (inner_rotated,) = call(
        pre_kernel, [arr((TRUNC, CH, LANES), bf16)],
        [frames1, padded, scr((COEF, CH, LANES), f32), scr((TRUNC, CH, LANES), bf16), pltpu.SemaphoreType.DMA],
        [node, table, edge_source, edge_bin], 10**9, "pre", far_outs=1,
    )
    core = lax.axis_index("core").reshape(1)
    half = arr((PACKED // 2, LANES), bf16)
    conv_grad, message, keep, send = call(
        conv_kernel, [edges16, edges32, half, half],
        [scr((TRUNC, CH, WIDE), bf16), scr((TRUNC, CH, WIDE), f32), scr((2, PACKED // 2, LANES), bf16),
         scr((TRUNC, CH, WIDE), f32), scr((TRUNC, CH, WIDE), bf16), frames2, padded, scr((COEF, CH, WIDE), f32),
         pltpu.SemaphoreType.DMA((2,))],
        [core, from_lower, from_upper, cot, table, edge_target, edge_bin, in_targets, in_bins] + weights
        + [edge_scale, in_scale, inner_rotated], 10**10, "conv", scalars=1, hbm=1, far_outs=1,
    )

    pieces = lax.axis_size(PLANE)
    (joint,) = call(join_kernel, [half], [], [keep, swap_cores(send)], 10**6, "join")
    joint = joint.reshape(pieces, -1, LANES)
    piece = joint.shape[1:]
    parts = to_all(joint, PLANE)
    back_lower, back_upper, inner = call(
        input_kernel, [packed_shape, packed_shape, arr((TRUNC, CH, LANES), bf16)], [scr((TRUNC, CH, WIDE), bf16)],
        [conv_grad] + weights + [joint], 10**10, "inputs", far=1,
    )
    back_zero = from_behind(back_upper, graph, 1)
    back_one = from_behind(back_lower, graph, -1)
    updated, token = call(
        update_kernel, [arr((COEF, CH, LANES), bf16), mark],
        [frames2, padded, scr((COEF, CH, WIDE), bf16)],
        [node, table, message, edge_bin, edge_target, in_bins, in_targets, inner], 10**10, "update", far=1,
    )
    feature_grad, token = call(
        back_kernel, [arr((COEF, CH, LANES), f32), mark],
        [frames2, frames1, padded, scr((TRUNC, SUB, WIDE), bf16), scr((COEF, SUB, WIDE), bf16),
         scr((COEF, CH, LANES), bf16)],
        [back_zero, back_one, inner, table, out_bins, out_atoms, edge_bin, edge_source, cot, token], 10**10,
        "back", far=1,
    )
    layers = lax.axis_size("z")
    (copies,) = call(add_kernel, [arr((layers,) + piece, bf16)], [], [parts, token], 10**7, "add_plane", far=1)
    sums = to_all(copies, "z")
    (copies,) = call(add_kernel, [arr((pieces,) + piece, bf16)], [], [sums, token], 10**7, "add_z", far=1)
    mine = to_all(copies, PLANE)
    other = swap_cores(mine)
    grads = []
    for swapped, value in enumerate((mine, other)):
        grads = call(
            functools.partial(unpack_kernel, pieces, swapped), [arr(w.shape, f32) for w in weights],
            [scr(w.shape, f32) for w in weights] + [pltpu.SemaphoreType.DMA((3,))],
            [core, value.reshape(half.shape)] + list(grads), 10**7, "unpack", scalars=1, hbm=len(grads),
            far_outs=3, aliases={2 + index: index for index in range(len(grads))},
        )
    grad_zero, grad_one, grad_two = grads
    return updated[None], feature_grad[None], grad_zero, grad_one, grad_two


def solution(mesh):
    cores, rows, columns = SPLIT
    graph = mesh.shape["graph"]
    fine = jax.sharding.Mesh(mesh.devices.reshape(graph // cores, cores, rows, columns), ("z", "core", "x", "y"))
    dp, along = PLANE, ("z", "core")
    nodes, edges = P(dp, None, None, along), P(dp, along)
    in_specs = (nodes, nodes) + (P(),) * 4 + (edges,) * 4 + (P(dp, along, None),) * 5
    return jax.shard_map(
        body, mesh=fine, in_specs=in_specs, out_specs=(nodes, nodes, P(), P(), P()), check_vma=False
    )
```

```python
import functools

import jax
import jax.numpy as jnp
from jax import lax
from jax.experimental import pallas as pl
from jax.experimental.pallas import tpu as pltpu
from jax.sharding import PartitionSpec as P

COEF, TRUNC, CH, LANES = 49, 29, 64, 128
CAP, GROUPS, SUB = 32, 4, 16
WIDE = 2 * LANES
PAD_ROWS = 32
ZERO, PLUS1, MINUS1, PLUS2, MINUS2 = (0, 448), (448, 832), (832, 1216), (1216, 1536), (1536, 1856)
VMEM = 24 * 1024 * 1024
f32, bf16 = jnp.float32, jnp.bfloat16


def degree_rows(degree):
    rows = [degree]
    if degree >= 1:
        rows = rows + [6 + degree, 12 + degree]
    if degree >= 2:
        rows = rows + [17 + degree, 22 + degree]
    return rows


def dot(left, right):
    return jnp.dot(left, right, preferred_element_type=f32)


def dot_nt(left, right):
    return lax.dot_general(left, right, (((1,), (1,)), ((), ())), preferred_element_type=f32)


def dot_tn(left, right):
    return lax.dot_general(left, right, (((0,), (0,)), ((), ())), preferred_element_type=f32)


def iota(shape, axis):
    return lax.broadcasted_iota(jnp.int32, shape, axis)


def one_hot(index, value=1.0):
    lanes = index.shape[1]
    return jnp.where(iota((LANES, lanes), 0) == index, value, 0.0).astype(f32).astype(bf16)


def load_frames(frames, padded, wigner, bins):
    padded[:, 0:TRUNC, :] = wigner[...]
    lanes = bins.shape[1]
    found = dot(padded[...].reshape(COEF * PAD_ROWS, LANES), one_hot(bins))
    frames[...] = found.reshape(COEF, PAD_ROWS, lanes)


def rotate_into(frames, values, found, chunk):
    channels = values.shape[1]

    def step(index, carry):
        part = pl.ds(pl.multiple_of(index * chunk, chunk), chunk)
        for degree in range(7):
            rows = degree_rows(degree)
            total = {}
            for k in range(degree * degree, (degree + 1) * (degree + 1)):
                value = values[k, part, :].astype(f32)
                for row in rows:
                    term = frames[k, row : row + 1, :] * value
                    total[row] = term if row not in total else total[row] + term
            for row in rows:
                found[row, part, :] = total[row].astype(found.dtype)
        return carry

    lax.fori_loop(0, channels // chunk, step, 0)


def rotate_back(frames, values, found, chunk):
    channels = values.shape[1]

    def step(index, carry):
        part = pl.ds(pl.multiple_of(index * chunk, chunk), chunk)
        for degree in range(7):
            rows = degree_rows(degree)
            held = {row: values[row, part, :].astype(f32) for row in rows}
            for k in range(degree * degree, (degree + 1) * (degree + 1)):
                total = None
                for row in rows:
                    term = frames[k, row : row + 1, :] * held[row]
                    total = term if total is None else total + term
                found[k, part, :] = total.astype(found.dtype)
        return carry

    lax.fori_loop(0, channels // chunk, step, 0)


def flat(value):
    return value.reshape(value.shape[0] * value.shape[1], value.shape[2])


def halo_row(pair, fill):
    rest = jnp.full((1, LANES - 2 * CAP), fill, pair.dtype)
    return jnp.concatenate([pair[0:1, :], pair[1:2, :], rest], axis=1)


def packed_row(pair):
    pieces = [pair[slot : slot + 1, :] for slot in range(2) for _ in range(GROUPS)]
    return jnp.concatenate(pieces, axis=1)


def rim_kernel(
    core, node_far, wigner_far, atoms_far, bins_far, to_lower, to_upper, node, wigner,
    frames, padded, gathered, rotated, atoms, bins, sems,
):
    pairs = [(wigner_far, wigner), (bins_far, bins), (atoms_far, atoms), (node_far, node)]
    copies = [pltpu.make_async_copy(far, near, sems.at[index]) for index, (far, near) in enumerate(pairs)]
    for copy in copies:
        copy.start()
    for copy in copies[0:3]:
        copy.wait()
    load_frames(frames, padded, wigner, packed_row(bins[...]))
    copies[3].wait()
    row = packed_row(atoms[...])
    wide = 2 * LANES
    group = (iota((GROUPS * LANES, wide), 1) & (LANES - 1)) >> 5
    entry = iota((GROUPS * LANES, wide), 0)
    table = jnp.where(entry == row + group * LANES, 1.0, 0.0).astype(f32).astype(bf16)
    left = jnp.concatenate(
        [flat(node[:, g * SUB : (g + 1) * SUB, :]) for g in range(GROUPS)], axis=1
    )
    gathered[...] = dot(left, table).reshape(COEF, SUB, wide)
    rotate_into(frames, gathered, rotated, SUB)
    to_lower[...] = rotated[:, :, 0:LANES]
    to_upper[...] = rotated[:, :, LANES:wide]


def pre_kernel(
    node, cot, wigner, sources, targets, bins, halo_targets, halo_bins,
    rotated, message_grad, frames, padded, values,
):
    joint_bins = jnp.concatenate([bins[...], halo_row(halo_bins[...], -1)], axis=1)
    joint_targets = jnp.concatenate([targets[...], halo_row(halo_targets[...], -1)], axis=1)
    load_frames(frames, padded, wigner, joint_bins)
    inner = slice(0, LANES)
    values[:, :, inner] = dot(flat(node[...]), one_hot(sources[...])).reshape(COEF, CH, LANES)
    rotate_into(frames.at[:, :, inner], values.at[:, :, inner], rotated, 32)
    values[...] = dot(flat(cot[...]), one_hot(joint_targets, 0.5)).reshape(COEF, CH, WIDE)
    rotate_into(frames, values, message_grad, 16)


def rows_of(values, first, last):
    return flat(values[first[0] // CH : last[1] // CH])


def conv_forward(rotated, conv, w_zero, w_one, w_two):
    def put(span, value):
        conv[span[0] // CH : span[1] // CH] = value.reshape(-1, CH, WIDE)

    put(ZERO, dot(w_zero[...], rows_of(rotated, ZERO, ZERO)))
    both = rows_of(rotated, PLUS1, MINUS1)
    put(PLUS1, dot(jnp.concatenate([w_one[0], -w_one[1]], axis=1), both))
    put(MINUS1, dot(jnp.concatenate([w_one[1], w_one[0]], axis=1), both))
    plus, minus = rows_of(rotated, PLUS2, PLUS2), rows_of(rotated, MINUS2, MINUS2)
    put(PLUS2, dot(w_two[0], plus) - dot(w_two[1], minus))
    put(MINUS2, dot(w_two[1], plus) + dot(w_two[0], minus))


def spread_table():
    shape = (2 * LANES, GROUPS * LANES)
    lane, column = iota(shape, 0), iota(shape, 1)
    slot, where = lane >> 7, lane & (LANES - 1)
    group, inside = column >> 7, column & (LANES - 1)
    same = (where >> 5 == group) & (inside == slot * CAP + (where & (CAP - 1)))
    return jnp.where(same, 1.0, 0.0).astype(f32).astype(bf16)


def pack_grads(packed, values):
    at = 0
    for value in values:
        height, width = value.shape
        for first in range(0, width - LANES + 1, LANES):
            packed[at : at + height, :] = value[:, first : first + LANES].astype(bf16)
            at += height
        if width % LANES:
            first, half = width - width % LANES, height // 2
            piece = value[:, first:width]
            packed[at : at + half, :] = jnp.concatenate([piece[0:half], piece[half:]], axis=1).astype(bf16)
            at += half
    packed[at:, :] = jnp.zeros((packed.shape[0] - at, LANES), bf16)


def conv_kernel(
    core, from_lower, from_upper, inner_rotated, message_grad, w_zero, w_one, w_two, scale, halo_scale,
    conv_grad_far, message, keep, send,
    rotated, conv, packed, conv_grad, sem,
):
    rotated[:, :, 0:LANES] = inner_rotated[...]
    left = jnp.concatenate([flat(from_lower[...]), flat(from_upper[...])], axis=1)
    spread = dot(left, spread_table()).astype(bf16)
    for g in range(GROUPS):
        rotated[:, g * SUB : (g + 1) * SUB, LANES:WIDE] = spread[:, g * LANES : (g + 1) * LANES].reshape(
            TRUNC, SUB, LANES
        )
    conv_forward(rotated, conv, w_zero, w_one, w_two)
    weight = jnp.concatenate([scale[...], halo_row(halo_scale[...], 0.0)], axis=1)
    gating = jax.nn.sigmoid(conv[0])
    factor = gating * weight
    factor_grad = message_grad[0] * conv[0]
    for row in range(1, TRUNC):
        value = conv[row]
        grad = message_grad[row]
        factor_grad = factor_grad + grad * value
        conv_grad[row] = (grad * factor).astype(bf16)
        message[row] = value * factor
    conv_grad[0] = (message_grad[0] * factor + factor_grad * weight * gating * (1.0 - gating)).astype(bf16)
    message[0] = conv[0] * factor
    put = pltpu.make_async_copy(conv_grad, conv_grad_far, sem)
    put.start()

    zero = dot_nt(rows_of(conv_grad, ZERO, ZERO), rows_of(rotated, ZERO, ZERO))
    pairs = []
    for plus, minus in ((PLUS1, MINUS1), (PLUS2, MINUS2)):
        g_plus, g_minus = rows_of(conv_grad, plus, plus), rows_of(conv_grad, minus, minus)
        inputs = jnp.concatenate([rows_of(rotated, plus, plus), rows_of(rotated, minus, minus)], axis=1)
        pairs.append([
            dot_nt(jnp.concatenate([g_plus, g_minus], axis=1), inputs),
            dot_nt(jnp.concatenate([g_minus, -g_plus], axis=1), inputs),
        ])
    one, two = pairs
    pack_grads(packed.at[0], [zero, one[0]])
    pack_grads(packed.at[1], [one[1]] + two)
    keep[...] = packed[core[0]]
    send[...] = packed[1 - core[0]]
    put.wait()


def input_kernel(conv_grad, w_zero, w_one, w_two, after, to_lower, to_upper, inner, joint):
    def put(span, value):
        joint[span[0] // CH : span[1] // CH] = value.astype(bf16).reshape(-1, CH, WIDE)

    put(ZERO, dot_tn(w_zero[...], rows_of(conv_grad, ZERO, ZERO)))
    for weights, plus, minus in ((w_one, PLUS1, MINUS1), (w_two, PLUS2, MINUS2)):
        both = flat(weights[...])
        put(plus, dot_tn(both, rows_of(conv_grad, plus, minus)))
        crossed = jnp.concatenate([rows_of(conv_grad, minus, minus), -rows_of(conv_grad, plus, plus)], axis=0)
        put(minus, dot_tn(both, crossed))
    left = jnp.concatenate(
        [flat(joint[:, g * SUB : (g + 1) * SUB, LANES:WIDE]) for g in range(GROUPS)], axis=1
    )
    shape = (GROUPS * LANES, WIDE)
    column, lane = iota(shape, 0), iota(shape, 1)
    slot, where = lane >> 7, lane & (LANES - 1)
    group, inside = column >> 7, column & (LANES - 1)
    same = (where >> 5 == group) & (inside == slot * CAP + (where & (CAP - 1)))
    gathered = dot(left, jnp.where(same, 1.0, 0.0).astype(f32).astype(bf16)).astype(bf16)
    to_lower[...] = gathered[:, 0:LANES].reshape(TRUNC, SUB, LANES)
    to_upper[...] = gathered[:, LANES:WIDE].reshape(TRUNC, SUB, LANES)
    inner[...] = joint[:, :, 0:LANES]


def update_kernel(
    node, wigner, message, bins, targets, halo_bins, halo_targets, after,
    updated, token, frames, padded, part,
):
    joint_bins = jnp.concatenate([bins[...], halo_row(halo_bins[...], -1)], axis=1)
    joint_targets = jnp.concatenate([targets[...], halo_row(halo_targets[...], -1)], axis=1)
    load_frames(frames, padded, wigner, joint_bins)
    rotate_back(frames, message, part, 16)
    summed = dot_nt(flat(part[...]), one_hot(joint_targets, 0.5)).reshape(COEF, CH, LANES)
    updated[...] = (node[...].astype(f32) + summed).astype(bf16)
    token[...] = jnp.zeros(token.shape, token.dtype)


def back_kernel(
    back_zero, back_one, inner, wigner, rim_bins, atoms, bins, sources, cot, after, feature_grad, token,
    frames, inner_frames, padded, joint, rim_grad, inner_grad,
):
    load_frames(inner_frames, padded, wigner, bins[...])
    rotate_back(inner_frames, inner, inner_grad, 32)
    load_frames(frames, padded, wigner, packed_row(rim_bins[...]))
    joint[:, :, 0:LANES] = back_zero[...]
    joint[:, :, LANES:WIDE] = back_one[...]
    rotate_back(frames, joint, rim_grad, SUB)
    row = packed_row(atoms[...])
    group = (iota((LANES, WIDE), 1) & (LANES - 1)) >> 5
    entry = iota((LANES, WIDE), 0)
    values = flat(rim_grad[...])
    inner_table = one_hot(sources[...])
    for g in range(GROUPS):
        part = slice(g * SUB, (g + 1) * SUB)
        table = jnp.where((entry == row) & (group == g), 1.0, 0.0).astype(f32).astype(bf16)
        scattered = dot_nt(values, table) + dot_nt(flat(inner_grad[:, part, :]), inner_table)
        feature_grad[:, part, :] = cot[:, part, :].astype(f32) + scattered.reshape(COEF, SUB, LANES)
    token[...] = jnp.zeros(token.shape, token.dtype)


def add_kernel(pieces, after, total):
    found = pieces[0].astype(f32)
    for index in range(1, pieces.shape[0]):
        found = found + pieces[index].astype(f32)
    found = found.astype(bf16)
    if total.ndim == 2:
        total[...] = found
    else:
        for index in range(total.shape[0]):
            total[index] = found


def join_kernel(keep, other, joint):
    joint[...] = (keep[...].astype(f32) + other[...].astype(f32)).astype(bf16)


def unpack_kernel(replicas, swapped, which, packed, *refs):
    (zero, one, two), (zero_v, one_v, two_v), sems = refs[-7:-4], refs[-4:-1], refs[-1]

    def write(pairs):
        at = 0
        copies = []
        for index, (ref, out) in enumerate(pairs):
            height, width = ref.shape
            for first in range(0, width - LANES + 1, LANES):
                ref[:, first : first + LANES] = packed[at : at + height, :].astype(f32) * (1.0 / replicas)
                at += height
            if width % LANES:
                first, part = width - width % LANES, height // 2
                value = packed[at : at + part, :].astype(f32) * (1.0 / replicas)
                ref[0:part, first:width] = value[:, 0 : width - first]
                ref[part:height, first:width] = value[:, width - first :]
                at += part
            copy = pltpu.make_async_copy(ref, out, sems.at[index])
            copy.start()
            copies.append(copy)
        for copy in copies:
            copy.wait()

    half = 1 - which[0] if swapped else which[0]

    @pl.when(half == 0)
    def first():
        write([(zero_v, zero), (one_v.at[0], one.at[0])])

    @pl.when(half == 1)
    def second():
        write([(one_v.at[1], one.at[1]), (two_v.at[0], two.at[0]), (two_v.at[1], two.at[1])])


def call(kernel, outs, scratch, operands, flops, name, scalars=0, far=0, hbm=0, far_outs=0, aliases=None):
    whole = pl.BlockSpec(memory_space=pltpu.VMEM)
    scalar = pl.BlockSpec(memory_space=pltpu.SMEM)
    away = pl.BlockSpec(memory_space=pl.ANY)
    main = pl.BlockSpec(memory_space=pltpu.HBM)
    moved = sum(v.size * v.dtype.itemsize for v in list(operands) + list(outs))
    operands = list(operands)
    for index in range(len(operands) - hbm, len(operands)):
        operands[index] = pltpu.with_memory_space_constraint(operands[index], pltpu.HBM)
    outs = [pltpu.HBM(v.shape, v.dtype) if index < far_outs else v for index, v in enumerate(outs)]
    near = len(operands) - scalars - far - hbm
    return pl.pallas_call(
        kernel,
        out_shape=tuple(outs),
        in_specs=[scalar] * scalars + [whole] * near + [away] * far + [main] * hbm,
        out_specs=tuple([main] * far_outs + [whole] * (len(outs) - far_outs)),
        scratch_shapes=scratch,
        input_output_aliases=aliases or {},
        compiler_params=pltpu.CompilerParams(vmem_limit_bytes=VMEM),
        cost_estimate=pl.CostEstimate(flops=flops, bytes_accessed=moved, transcendentals=0),
        name=name,
    )(*operands)


def arr(shape, dtype):
    return jax.ShapeDtypeStruct(shape, dtype)


def scr(shape, dtype):
    return pltpu.VMEM(shape, dtype)


def from_behind(value, axis, steps):
    count = lax.axis_size(axis)
    return lax.ppermute(value, axis, [(source, (source + steps) % count) for source in range(count)])


def swap_cores(value):
    return lax.ppermute(value, "core", [(0, 1), (1, 0)])


def to_all(copies, axes):
    return lax.all_to_all(copies, axes, 0, 0)


PACKED = 5632
SPLIT = (2, 4, 8)
PLANE = ("x", "y")


def body(
    node_features, cotangent, wigner, w_zero, w_one, w_two, edge_source, edge_target, edge_bin, edge_scale,
    send_atoms, send_bins, recv_targets, recv_bins, recv_scale,
):
    node, cot = node_features[0], cotangent[0]
    table = jnp.transpose(wigner, (2, 1, 0))
    graph = ("z", "core")
    out_atoms, out_bins = send_atoms[0], send_bins[0]
    in_targets, in_bins, in_scale = recv_targets[0], recv_bins[0], recv_scale[0]
    weights = [w_zero, w_one, w_two]
    packed_shape = arr((TRUNC, SUB, LANES), bf16)
    edges16, edges32 = arr((TRUNC, CH, WIDE), bf16), arr((TRUNC, CH, WIDE), f32)
    frames1, frames2 = scr((COEF, PAD_ROWS, LANES), f32), scr((COEF, PAD_ROWS, WIDE), f32)
    padded = scr((COEF, PAD_ROWS, LANES), bf16)
    mark = arr((8, LANES), f32)

    core = lax.axis_index("core").reshape(1)
    to_lower, to_upper, near_node, near_table = call(
        rim_kernel, [packed_shape] * 2 + [arr(node.shape, bf16), arr(table.shape, bf16)],
        [frames2, padded, scr((COEF, SUB, WIDE), f32), scr((TRUNC, SUB, WIDE), bf16),
         scr(out_atoms.shape, jnp.int32),
         scr(out_bins.shape, jnp.int32), pltpu.SemaphoreType.DMA((4,))],
        [core, node, table, out_atoms, out_bins], 10**9, "rim", scalars=1, hbm=4,
    )
    from_lower = from_behind(to_upper, graph, 1)
    from_upper = from_behind(to_lower, graph, -1)
    inner_rotated, message_grad = call(
        pre_kernel, [arr((TRUNC, CH, LANES), bf16), edges32],
        [frames2, padded, scr((COEF, CH, WIDE), f32)],
        [near_node, cot, near_table, edge_source, edge_target, edge_bin, in_targets, in_bins], 10**10, "pre",
    )
    half = arr((PACKED // 2, LANES), bf16)
    conv_grad, message, keep, send = call(
        conv_kernel, [edges16, edges32, half, half],
        [scr((TRUNC, CH, WIDE), bf16), scr((TRUNC, CH, WIDE), f32), scr((2, PACKED // 2, LANES), bf16),
         scr((TRUNC, CH, WIDE), bf16), pltpu.SemaphoreType.DMA],
        [core, from_lower, from_upper, inner_rotated, message_grad] + weights + [edge_scale, in_scale],
        10**10, "conv", scalars=1, far_outs=1,
    )

    pieces = lax.axis_size(PLANE)
    (joint,) = call(join_kernel, [half], [], [keep, swap_cores(send)], 10**6, "join")
    joint = joint.reshape(pieces, -1, LANES)
    piece = joint.shape[1:]
    parts = to_all(joint, PLANE)
    back_lower, back_upper, inner = call(
        input_kernel, [packed_shape, packed_shape, arr((TRUNC, CH, LANES), bf16)], [scr((TRUNC, CH, WIDE), bf16)],
        [conv_grad] + weights + [joint], 10**10, "inputs", far=1,
    )
    back_zero = from_behind(back_upper, graph, 1)
    back_one = from_behind(back_lower, graph, -1)
    updated, token = call(
        update_kernel, [arr((COEF, CH, LANES), bf16), mark],
        [frames2, padded, scr((COEF, CH, WIDE), bf16)],
        [node, table, message, edge_bin, edge_target, in_bins, in_targets, inner], 10**10, "update", far=1,
    )
    feature_grad, token = call(
        back_kernel, [arr((COEF, CH, LANES), f32), mark],
        [frames2, frames1, padded, scr((TRUNC, SUB, WIDE), bf16), scr((COEF, SUB, WIDE), bf16),
         scr((COEF, CH, LANES), bf16)],
        [back_zero, back_one, inner, table, out_bins, out_atoms, edge_bin, edge_source, cot, token], 10**10,
        "back", far=1,
    )
    layers = lax.axis_size("z")
    (copies,) = call(add_kernel, [arr((layers,) + piece, bf16)], [], [parts, token], 10**7, "add_plane", far=1)
    sums = to_all(copies, "z")
    (copies,) = call(add_kernel, [arr((pieces,) + piece, bf16)], [], [sums, token], 10**7, "add_z", far=1)
    mine = to_all(copies, PLANE)
    other = swap_cores(mine)
    grads = []
    for swapped, value in enumerate((mine, other)):
        grads = call(
            functools.partial(unpack_kernel, pieces, swapped), [arr(w.shape, f32) for w in weights],
            [scr(w.shape, f32) for w in weights] + [pltpu.SemaphoreType.DMA((3,))],
            [core, value.reshape(half.shape)] + list(grads), 10**7, "unpack", scalars=1, hbm=len(grads),
            far_outs=3, aliases={2 + index: index for index in range(len(grads))},
        )
    grad_zero, grad_one, grad_two = grads
    return updated[None], feature_grad[None], grad_zero, grad_one, grad_two


def solution(mesh):
    cores, rows, columns = SPLIT
    graph = mesh.shape["graph"]
    fine = jax.sharding.Mesh(mesh.devices.reshape(graph // cores, cores, rows, columns), ("z", "core", "x", "y"))
    dp, along = PLANE, ("z", "core")
    nodes, edges = P(dp, None, None, along), P(dp, along)
    in_specs = (nodes, nodes) + (P(),) * 4 + (edges,) * 4 + (P(dp, along, None),) * 5
    return jax.shard_map(
        body, mesh=fine, in_specs=in_specs, out_specs=(nodes, nodes, P(), P(), P()), check_vma=False
    )
```

```python
import functools

import jax
import jax.numpy as jnp
from jax import lax
from jax.experimental import pallas as pl
from jax.experimental.pallas import tpu as pltpu
from jax.sharding import PartitionSpec as P

COEF, TRUNC, CH, LANES = 49, 29, 64, 128
CAP, GROUPS, SUB = 32, 4, 16
WIDE = 2 * LANES
PAD_ROWS = 32
ZERO, PLUS1, MINUS1, PLUS2, MINUS2 = (0, 448), (448, 832), (832, 1216), (1216, 1536), (1536, 1856)
VMEM = 24 * 1024 * 1024
f32, bf16 = jnp.float32, jnp.bfloat16


def degree_rows(degree):
    rows = [degree]
    if degree >= 1:
        rows = rows + [6 + degree, 12 + degree]
    if degree >= 2:
        rows = rows + [17 + degree, 22 + degree]
    return rows


def dot(left, right):
    return jnp.dot(left, right, preferred_element_type=f32)


def dot_nt(left, right):
    return lax.dot_general(left, right, (((1,), (1,)), ((), ())), preferred_element_type=f32)


def dot_tn(left, right):
    return lax.dot_general(left, right, (((0,), (0,)), ((), ())), preferred_element_type=f32)


def iota(shape, axis):
    return lax.broadcasted_iota(jnp.int32, shape, axis)


def one_hot(index, value=1.0):
    lanes = index.shape[1]
    return jnp.where(iota((LANES, lanes), 0) == index, value, 0.0).astype(f32).astype(bf16)


def load_frames(frames, padded, wigner, bins):
    padded[:, 0:TRUNC, :] = wigner[...]
    lanes = bins.shape[1]
    found = dot(padded[...].reshape(COEF * PAD_ROWS, LANES), one_hot(bins))
    frames[...] = found.reshape(COEF, PAD_ROWS, lanes)


def rotate_into(frames, values, found, chunk):
    channels = values.shape[1]

    def step(index, carry):
        part = pl.ds(pl.multiple_of(index * chunk, chunk), chunk)
        for degree in range(7):
            rows = degree_rows(degree)
            total = {}
            for k in range(degree * degree, (degree + 1) * (degree + 1)):
                value = values[k, part, :].astype(f32)
                for row in rows:
                    term = frames[k, row : row + 1, :] * value
                    total[row] = term if row not in total else total[row] + term
            for row in rows:
                found[row, part, :] = total[row].astype(found.dtype)
        return carry

    lax.fori_loop(0, channels // chunk, step, 0)


def rotate_back(frames, values, found, chunk):
    channels = values.shape[1]

    def step(index, carry):
        part = pl.ds(pl.multiple_of(index * chunk, chunk), chunk)
        for degree in range(7):
            rows = degree_rows(degree)
            held = {row: values[row, part, :].astype(f32) for row in rows}
            for k in range(degree * degree, (degree + 1) * (degree + 1)):
                total = None
                for row in rows:
                    term = frames[k, row : row + 1, :] * held[row]
                    total = term if total is None else total + term
                found[k, part, :] = total.astype(found.dtype)
        return carry

    lax.fori_loop(0, channels // chunk, step, 0)


def flat(value):
    return value.reshape(value.shape[0] * value.shape[1], value.shape[2])


def halo_row(pair, fill):
    rest = jnp.full((1, LANES - 2 * CAP), fill, pair.dtype)
    return jnp.concatenate([pair[0:1, :], pair[1:2, :], rest], axis=1)


def packed_row(pair):
    pieces = [pair[slot : slot + 1, :] for slot in range(2) for _ in range(GROUPS)]
    return jnp.concatenate(pieces, axis=1)


def rim_kernel(
    core, node_far, wigner_far, atoms_far, bins_far, outer, inner, node, wigner,
    frames, padded, gathered, rotated, atoms, bins, sems,
):
    pairs = [(wigner_far, wigner), (bins_far, bins), (atoms_far, atoms), (node_far, node)]
    copies = [pltpu.make_async_copy(far, near, sems.at[index]) for index, (far, near) in enumerate(pairs)]
    for copy in copies:
        copy.start()
    for copy in copies[0:3]:
        copy.wait()
    load_frames(frames, padded, wigner, packed_row(bins[...]))
    copies[3].wait()
    row = packed_row(atoms[...])
    wide = 2 * LANES
    group = (iota((GROUPS * LANES, wide), 1) & (LANES - 1)) >> 5
    entry = iota((GROUPS * LANES, wide), 0)
    table = jnp.where(entry == row + group * LANES, 1.0, 0.0).astype(f32).astype(bf16)
    left = jnp.concatenate(
        [flat(node[:, g * SUB : (g + 1) * SUB, :]) for g in range(GROUPS)], axis=1
    )
    gathered[...] = dot(left, table).reshape(COEF, SUB, wide)
    rotate_into(frames, gathered, rotated, SUB)
    outer[...] = rotated[:, :, pl.ds(pl.multiple_of(core[0] * LANES, LANES), LANES)]
    inner[...] = rotated[:, :, pl.ds(pl.multiple_of((1 - core[0]) * LANES, LANES), LANES)]


def pre_kernel(
    node, cot, wigner, sources, targets, bins, halo_targets, halo_bins,
    rotated, message_grad, frames, padded, values,
):
    joint_bins = jnp.concatenate([bins[...], halo_row(halo_bins[...], -1)], axis=1)
    joint_targets = jnp.concatenate([targets[...], halo_row(halo_targets[...], -1)], axis=1)
    load_frames(frames, padded, wigner, joint_bins)
    inner, halo = slice(0, LANES), slice(LANES, WIDE)
    values[:, :, inner] = dot(flat(node[...]), one_hot(sources[...])).reshape(COEF, CH, LANES)
    rotate_into(frames.at[:, :, inner], values.at[:, :, inner], rotated, CH)
    table = one_hot(joint_targets, 0.5)
    for part in (inner, halo):
        values[:, :, part] = dot(flat(cot[...]), table[:, part]).reshape(COEF, CH, LANES)
        rotate_into(frames.at[:, :, part], values.at[:, :, part], message_grad.at[:, :, part], CH)


def rows_of(values, first, last):
    return flat(values[first[0] // CH : last[1] // CH])


def conv_forward(rotated, conv, w_zero, w_one, w_two):
    def put(span, value):
        conv[span[0] // CH : span[1] // CH] = value.reshape(-1, CH, WIDE)

    put(ZERO, dot(w_zero[...], rows_of(rotated, ZERO, ZERO)))
    both = rows_of(rotated, PLUS1, MINUS1)
    put(PLUS1, dot(jnp.concatenate([w_one[0], -w_one[1]], axis=1), both))
    put(MINUS1, dot(jnp.concatenate([w_one[1], w_one[0]], axis=1), both))
    plus, minus = rows_of(rotated, PLUS2, PLUS2), rows_of(rotated, MINUS2, MINUS2)
    put(PLUS2, dot(w_two[0], plus) - dot(w_two[1], minus))
    put(MINUS2, dot(w_two[1], plus) + dot(w_two[0], minus))


def spread_table():
    shape = (2 * LANES, GROUPS * LANES)
    lane, column = iota(shape, 0), iota(shape, 1)
    slot, where = lane >> 7, lane & (LANES - 1)
    group, inside = column >> 7, column & (LANES - 1)
    same = (where >> 5 == group) & (inside == slot * CAP + (where & (CAP - 1)))
    return jnp.where(same, 1.0, 0.0).astype(f32).astype(bf16)


def pack_grads(packed, values):
    at = 0
    for value in values:
        height, width = value.shape
        for first in range(0, width - LANES + 1, LANES):
            packed[at : at + height, :] = value[:, first : first + LANES].astype(bf16)
            at += height
        if width % LANES:
            first, half = width - width % LANES, height // 2
            piece = value[:, first:width]
            packed[at : at + half, :] = jnp.concatenate([piece[0:half], piece[half:]], axis=1).astype(bf16)
            at += half
    packed[at:, :] = jnp.zeros((packed.shape[0] - at, LANES), bf16)


def conv_kernel(
    core, outer, inner, inner_rotated, message_grad, w_zero, w_one, w_two, scale, halo_scale,
    conv_grad, message, keep, send,
    rotated, conv, packed, halo,
):
    rotated[:, :, 0:LANES] = inner_rotated[...]
    halo[core[0]] = flat(outer[...])
    halo[1 - core[0]] = flat(inner[...])
    left = jnp.concatenate([halo[0], halo[1]], axis=1)
    spread = dot(left, spread_table()).astype(bf16)
    for g in range(GROUPS):
        rotated[:, g * SUB : (g + 1) * SUB, LANES:WIDE] = spread[:, g * LANES : (g + 1) * LANES].reshape(
            TRUNC, SUB, LANES
        )
    conv_forward(rotated, conv, w_zero, w_one, w_two)
    weight = jnp.concatenate([scale[...], halo_row(halo_scale[...], 0.0)], axis=1)
    gating = jax.nn.sigmoid(conv[0])
    factor = gating * weight
    factor_grad = message_grad[0] * conv[0]
    for row in range(1, TRUNC):
        value = conv[row]
        grad = message_grad[row]
        factor_grad = factor_grad + grad * value
        conv_grad[row] = (grad * factor).astype(bf16)
        message[row] = value * factor
    conv_grad[0] = (message_grad[0] * factor + factor_grad * weight * gating * (1.0 - gating)).astype(bf16)
    message[0] = conv[0] * factor

    zero = dot_nt(rows_of(conv_grad, ZERO, ZERO), rows_of(rotated, ZERO, ZERO))
    pairs = []
    for plus, minus in ((PLUS1, MINUS1), (PLUS2, MINUS2)):
        g_plus, g_minus = rows_of(conv_grad, plus, plus), rows_of(conv_grad, minus, minus)
        inputs = jnp.concatenate([rows_of(rotated, plus, plus), rows_of(rotated, minus, minus)], axis=1)
        pairs.append([
            dot_nt(jnp.concatenate([g_plus, g_minus], axis=1), inputs),
            dot_nt(jnp.concatenate([g_minus, -g_plus], axis=1), inputs),
        ])
    one, two = pairs
    pack_grads(packed.at[0], [zero, one[0]])
    pack_grads(packed.at[1], [one[1]] + two)
    keep[...] = packed[core[0]]
    send[...] = packed[1 - core[0]]


def input_kernel(conv_grad, w_zero, w_one, w_two, after, to_lower, to_upper, inner, joint):
    def put(span, value):
        joint[span[0] // CH : span[1] // CH] = value.astype(bf16).reshape(-1, CH, WIDE)

    put(ZERO, dot_tn(w_zero[...], rows_of(conv_grad, ZERO, ZERO)))
    for weights, plus, minus in ((w_one, PLUS1, MINUS1), (w_two, PLUS2, MINUS2)):
        both = flat(weights[...])
        put(plus, dot_tn(both, rows_of(conv_grad, plus, minus)))
        crossed = jnp.concatenate([rows_of(conv_grad, minus, minus), -rows_of(conv_grad, plus, plus)], axis=0)
        put(minus, dot_tn(both, crossed))
    left = jnp.concatenate(
        [flat(joint[:, g * SUB : (g + 1) * SUB, LANES:WIDE]) for g in range(GROUPS)], axis=1
    )
    shape = (GROUPS * LANES, WIDE)
    column, lane = iota(shape, 0), iota(shape, 1)
    slot, where = lane >> 7, lane & (LANES - 1)
    group, inside = column >> 7, column & (LANES - 1)
    same = (where >> 5 == group) & (inside == slot * CAP + (where & (CAP - 1)))
    gathered = dot(left, jnp.where(same, 1.0, 0.0).astype(f32).astype(bf16)).astype(bf16)
    to_lower[...] = gathered[:, 0:LANES].reshape(TRUNC, SUB, LANES)
    to_upper[...] = gathered[:, LANES:WIDE].reshape(TRUNC, SUB, LANES)
    inner[...] = joint[:, :, 0:LANES]


def update_kernel(
    node, wigner, message, bins, targets, halo_bins, halo_targets, after,
    updated, token, frames, padded, part,
):
    joint_bins = jnp.concatenate([bins[...], halo_row(halo_bins[...], -1)], axis=1)
    joint_targets = jnp.concatenate([targets[...], halo_row(halo_targets[...], -1)], axis=1)
    load_frames(frames, padded, wigner, joint_bins)
    rotate_back(frames, message, part, 16)
    summed = dot_nt(flat(part[...]), one_hot(joint_targets, 0.5)).reshape(COEF, CH, LANES)
    updated[...] = (node[...].astype(f32) + summed).astype(bf16)
    token[...] = jnp.zeros(token.shape, token.dtype)


def back_kernel(
    back_zero, back_one, inner, wigner, rim_bins, atoms, bins, sources, cot, after, feature_grad, token,
    frames, inner_frames, padded, joint, rim_grad, inner_grad,
):
    load_frames(inner_frames, padded, wigner, bins[...])
    rotate_back(inner_frames, inner, inner_grad, 32)
    load_frames(frames, padded, wigner, packed_row(rim_bins[...]))
    joint[:, :, 0:LANES] = back_zero[...]
    joint[:, :, LANES:WIDE] = back_one[...]
    rotate_back(frames, joint, rim_grad, SUB)
    row = packed_row(atoms[...])
    group = (iota((LANES, WIDE), 1) & (LANES - 1)) >> 5
    entry = iota((LANES, WIDE), 0)
    values = flat(rim_grad[...])
    inner_table = one_hot(sources[...])
    for g in range(GROUPS):
        part = slice(g * SUB, (g + 1) * SUB)
        table = jnp.where((entry == row) & (group == g), 1.0, 0.0).astype(f32).astype(bf16)
        scattered = dot_nt(values, table) + dot_nt(flat(inner_grad[:, part, :]), inner_table)
        feature_grad[:, part, :] = cot[:, part, :].astype(f32) + scattered.reshape(COEF, SUB, LANES)
    token[...] = jnp.zeros(token.shape, token.dtype)


def add_kernel(pieces, after, total):
    found = pieces[0].astype(f32)
    for index in range(1, pieces.shape[0]):
        found = found + pieces[index].astype(f32)
    found = found.astype(bf16)
    if total.ndim == 2:
        total[...] = found
    else:
        for index in range(total.shape[0]):
            total[index] = found


def leave_kernel(conv_grad, message, conv_grad_far, message_far, token, sems):
    puts = [
        pltpu.make_async_copy(conv_grad, conv_grad_far, sems.at[0]),
        pltpu.make_async_copy(message, message_far, sems.at[1]),
    ]
    for put in puts:
        put.start()
    token[...] = jnp.zeros(token.shape, token.dtype)
    for put in puts:
        put.wait()


def join_kernel(keep, other, after, joint_far, joint, sems):
    count = sems.shape[0]
    rows = joint.shape[0] // count
    copies = []
    for index in range(count):
        part = slice(index * rows, (index + 1) * rows)
        joint[part, :] = (keep[part, :].astype(f32) + other[part, :].astype(f32)).astype(bf16)
        copies.append(pltpu.make_async_copy(joint.at[part, :], joint_far.at[part, :], sems.at[index]))
        copies[-1].start()
    for copy in copies:
        copy.wait()


def unpack_kernel(replicas, swapped, which, packed, *refs):
    (zero, one, two), (zero_v, one_v, two_v), sems = refs[-7:-4], refs[-4:-1], refs[-1]

    def write(pairs):
        at = 0
        copies = []
        for index, (ref, out) in enumerate(pairs):
            height, width = ref.shape
            for first in range(0, width - LANES + 1, LANES):
                ref[:, first : first + LANES] = packed[at : at + height, :].astype(f32) * (1.0 / replicas)
                at += height
            if width % LANES:
                first, part = width - width % LANES, height // 2
                value = packed[at : at + part, :].astype(f32) * (1.0 / replicas)
                ref[0:part, first:width] = value[:, 0 : width - first]
                ref[part:height, first:width] = value[:, width - first :]
                at += part
            copy = pltpu.make_async_copy(ref, out, sems.at[index])
            copy.start()
            copies.append(copy)
        for copy in copies:
            copy.wait()

    half = 1 - which[0] if swapped else which[0]

    @pl.when(half == 0)
    def first():
        write([(zero_v, zero), (one_v.at[0], one.at[0])])

    @pl.when(half == 1)
    def second():
        write([(one_v.at[1], one.at[1]), (two_v.at[0], two.at[0]), (two_v.at[1], two.at[1])])


def call(kernel, outs, scratch, operands, flops, name, scalars=0, far=0, hbm=0, far_outs=0, aliases=None):
    whole = pl.BlockSpec(memory_space=pltpu.VMEM)
    scalar = pl.BlockSpec(memory_space=pltpu.SMEM)
    away = pl.BlockSpec(memory_space=pl.ANY)
    main = pl.BlockSpec(memory_space=pltpu.HBM)
    moved = sum(v.size * v.dtype.itemsize for v in list(operands) + list(outs))
    operands = list(operands)
    for index in range(len(operands) - hbm, len(operands)):
        operands[index] = pltpu.with_memory_space_constraint(operands[index], pltpu.HBM)
    outs = [pltpu.HBM(v.shape, v.dtype) if index < far_outs else v for index, v in enumerate(outs)]
    near = len(operands) - scalars - far - hbm
    return pl.pallas_call(
        kernel,
        out_shape=tuple(outs),
        in_specs=[scalar] * scalars + [whole] * near + [away] * far + [main] * hbm,
        out_specs=tuple([main] * far_outs + [whole] * (len(outs) - far_outs)),
        scratch_shapes=scratch,
        input_output_aliases=aliases or {},
        compiler_params=pltpu.CompilerParams(vmem_limit_bytes=VMEM),
        cost_estimate=pl.CostEstimate(flops=flops, bytes_accessed=moved, transcendentals=0),
        name=name,
    )(*operands)


def arr(shape, dtype):
    return jax.ShapeDtypeStruct(shape, dtype)


def scr(shape, dtype):
    return pltpu.VMEM(shape, dtype)


def from_behind(value, axis, steps):
    count = lax.axis_size(axis)
    return lax.ppermute(value, axis, [(source, (source + steps) % count) for source in range(count)])


def across_chips(value):
    chips = lax.axis_size("z")
    pairs = []
    for chip in range(chips):
        pairs += [(2 * chip, (2 * chip - 1) % (2 * chips)), (2 * chip + 1, (2 * chip + 2) % (2 * chips))]
    return lax.ppermute(value, ("z", "core"), pairs)


def swap_cores(value):
    return lax.ppermute(value, "core", [(0, 1), (1, 0)])


def to_all(copies, axes):
    return lax.all_to_all(copies, axes, 0, 0)


PACKED = 5632
SPLIT = (2, 4, 8)
PLANE = ("x", "y")


def body(
    node_features, cotangent, wigner, w_zero, w_one, w_two, edge_source, edge_target, edge_bin, edge_scale,
    send_atoms, send_bins, recv_targets, recv_bins, recv_scale,
):
    node, cot = node_features[0], cotangent[0]
    table = jnp.transpose(wigner, (2, 1, 0))
    graph = ("z", "core")
    out_atoms, out_bins = send_atoms[0], send_bins[0]
    in_targets, in_bins, in_scale = recv_targets[0], recv_bins[0], recv_scale[0]
    weights = [w_zero, w_one, w_two]
    packed_shape = arr((TRUNC, SUB, LANES), bf16)
    edges16, edges32 = arr((TRUNC, CH, WIDE), bf16), arr((TRUNC, CH, WIDE), f32)
    frames1, frames2 = scr((COEF, PAD_ROWS, LANES), f32), scr((COEF, PAD_ROWS, WIDE), f32)
    padded = scr((COEF, PAD_ROWS, LANES), bf16)
    mark = arr((8, LANES), f32)

    core = lax.axis_index("core").reshape(1)
    outer, inner, near_node, near_table = call(
        rim_kernel, [packed_shape] * 2 + [arr(node.shape, bf16), arr(table.shape, bf16)],
        [frames2, padded, scr((COEF, SUB, WIDE), f32), scr((TRUNC, SUB, WIDE), bf16),
         scr(out_atoms.shape, jnp.int32),
         scr(out_bins.shape, jnp.int32), pltpu.SemaphoreType.DMA((4,))],
        [core, node, table, out_atoms, out_bins], 10**9, "rim", scalars=1, hbm=4,
    )
    outer, inner = across_chips(outer), swap_cores(inner)
    inner_rotated, message_grad = call(
        pre_kernel, [arr((TRUNC, CH, LANES), bf16), edges32],
        [frames2, padded, scr((COEF, CH, WIDE), f32)],
        [near_node, cot, near_table, edge_source, edge_target, edge_bin, in_targets, in_bins], 10**10, "pre",
    )
    half = arr((PACKED // 2, LANES), bf16)
    conv_grad, message, keep, send = call(
        conv_kernel, [edges16, edges32, half, half],
        [scr((TRUNC, CH, WIDE), bf16), scr((TRUNC, CH, WIDE), f32), scr((2, PACKED // 2, LANES), bf16),
         scr((2, TRUNC * SUB, LANES), bf16)],
        [core, outer, inner, inner_rotated, message_grad] + weights + [edge_scale, in_scale],
        10**10, "conv", scalars=1,
    )

    pieces = lax.axis_size(PLANE)
    other = swap_cores(send)
    conv_grad, message, token = call(
        leave_kernel, [edges16, edges32, mark], [pltpu.SemaphoreType.DMA((2,))], [conv_grad, message], 10**6, "leave",
        far_outs=2,
    )
    (joint,) = call(
        join_kernel, [half], [scr(half.shape, bf16), pltpu.SemaphoreType.DMA((4,))], [keep, other, token],
        10**6, "join", far=1, far_outs=1,
    )
    joint = joint.reshape(pieces, -1, LANES)
    piece = joint.shape[1:]
    parts = to_all(joint, PLANE)
    back_lower, back_upper, inner = call(
        input_kernel, [packed_shape, packed_shape, arr((TRUNC, CH, LANES), bf16)], [scr((TRUNC, CH, WIDE), bf16)],
        [conv_grad] + weights + [joint], 10**10, "inputs", far=1,
    )
    back_zero = from_behind(back_upper, graph, 1)
    back_one = from_behind(back_lower, graph, -1)
    updated, token = call(
        update_kernel, [arr((COEF, CH, LANES), bf16), mark],
        [frames2, padded, scr((COEF, CH, WIDE), bf16)],
        [node, table, message, edge_bin, edge_target, in_bins, in_targets, inner], 10**10, "update", far=1,
    )
    feature_grad, token = call(
        back_kernel, [arr((COEF, CH, LANES), f32), mark],
        [frames2, frames1, padded, scr((TRUNC, SUB, WIDE), bf16), scr((COEF, SUB, WIDE), bf16),
         scr((COEF, CH, LANES), bf16)],
        [back_zero, back_one, inner, table, out_bins, out_atoms, edge_bin, edge_source, cot, token], 10**10,
        "back", far=1,
    )
    layers = lax.axis_size("z")
    (copies,) = call(add_kernel, [arr((layers,) + piece, bf16)], [], [parts, token], 10**7, "add_plane", far=1)
    sums = to_all(copies, "z")
    (copies,) = call(add_kernel, [arr((pieces,) + piece, bf16)], [], [sums, token], 10**7, "add_z", far=1)
    mine = to_all(copies, PLANE)
    other = swap_cores(mine)
    grads = []
    for swapped, value in enumerate((mine, other)):
        grads = call(
            functools.partial(unpack_kernel, pieces, swapped), [arr(w.shape, f32) for w in weights],
            [scr(w.shape, f32) for w in weights] + [pltpu.SemaphoreType.DMA((3,))],
            [core, value.reshape(half.shape)] + list(grads), 10**7, "unpack", scalars=1, hbm=len(grads),
            far_outs=3, aliases={2 + index: index for index in range(len(grads))},
        )
    grad_zero, grad_one, grad_two = grads
    return updated[None], feature_grad[None], grad_zero, grad_one, grad_two


def solution(mesh):
    cores, rows, columns = SPLIT
    graph = mesh.shape["graph"]
    fine = jax.sharding.Mesh(mesh.devices.reshape(graph // cores, cores, rows, columns), ("z", "core", "x", "y"))
    dp, along = PLANE, ("z", "core")
    nodes, edges = P(dp, None, None, along), P(dp, along)
    in_specs = (nodes, nodes) + (P(),) * 4 + (edges,) * 4 + (P(dp, along, None),) * 5
    return jax.shard_map(
        body, mesh=fine, in_specs=in_specs, out_specs=(nodes, nodes, P(), P(), P()), check_vma=False
    )
```

```python
import functools

import jax
import jax.numpy as jnp
from jax import lax
from jax.experimental import pallas as pl
from jax.experimental.pallas import tpu as pltpu
from jax.sharding import PartitionSpec as P

COEF, TRUNC, CH, LANES = 49, 29, 64, 128
CAP, GROUPS, SUB = 32, 4, 16
WIDE = 2 * LANES
PAD_ROWS = 32
ZERO, PLUS1, MINUS1, PLUS2, MINUS2 = (0, 448), (448, 832), (832, 1216), (1216, 1536), (1536, 1856)
VMEM = 24 * 1024 * 1024
f32, bf16 = jnp.float32, jnp.bfloat16


def degree_rows(degree):
    rows = [degree]
    if degree >= 1:
        rows = rows + [6 + degree, 12 + degree]
    if degree >= 2:
        rows = rows + [17 + degree, 22 + degree]
    return rows


def dot(left, right):
    return jnp.dot(left, right, preferred_element_type=f32)


def dot_nt(left, right):
    return lax.dot_general(left, right, (((1,), (1,)), ((), ())), preferred_element_type=f32)


def dot_tn(left, right):
    return lax.dot_general(left, right, (((0,), (0,)), ((), ())), preferred_element_type=f32)


def iota(shape, axis):
    return lax.broadcasted_iota(jnp.int32, shape, axis)


def one_hot(index, value=1.0):
    lanes = index.shape[1]
    return jnp.where(iota((LANES, lanes), 0) == index, value, 0.0).astype(f32).astype(bf16)


def load_frames(frames, padded, wigner, bins):
    padded[:, 0:TRUNC, :] = wigner[...]
    lanes = bins.shape[1]
    found = dot(padded[...].reshape(COEF * PAD_ROWS, LANES), one_hot(bins))
    frames[...] = found.reshape(COEF, PAD_ROWS, lanes)


def rotate_into(frames, values, found, chunk):
    channels = values.shape[1]

    def step(index, carry):
        part = pl.ds(pl.multiple_of(index * chunk, chunk), chunk)
        for degree in range(7):
            rows = degree_rows(degree)
            total = {}
            for k in range(degree * degree, (degree + 1) * (degree + 1)):
                value = values[k, part, :].astype(f32)
                for row in rows:
                    term = frames[k, row : row + 1, :] * value
                    total[row] = term if row not in total else total[row] + term
            for row in rows:
                found[row, part, :] = total[row].astype(found.dtype)
        return carry

    lax.fori_loop(0, channels // chunk, step, 0)


def rotate_back(frames, values, found, chunk):
    channels = values.shape[1]

    def step(index, carry):
        part = pl.ds(pl.multiple_of(index * chunk, chunk), chunk)
        for degree in range(7):
            rows = degree_rows(degree)
            held = {row: values[row, part, :].astype(f32) for row in rows}
            for k in range(degree * degree, (degree + 1) * (degree + 1)):
                total = None
                for row in rows:
                    term = frames[k, row : row + 1, :] * held[row]
                    total = term if total is None else total + term
                found[k, part, :] = total.astype(found.dtype)
        return carry

    lax.fori_loop(0, channels // chunk, step, 0)


def flat(value):
    return value.reshape(value.shape[0] * value.shape[1], value.shape[2])


def halo_row(pair, fill):
    rest = jnp.full((1, LANES - 2 * CAP), fill, pair.dtype)
    return jnp.concatenate([pair[0:1, :], pair[1:2, :], rest], axis=1)


def packed_row(pair):
    pieces = [pair[slot : slot + 1, :] for slot in range(2) for _ in range(GROUPS)]
    return jnp.concatenate(pieces, axis=1)


def rim_kernel(
    core, node_far, wigner_far, atoms_far, bins_far, outer, inner, node, wigner,
    frames, padded, gathered, rotated, atoms, bins, sems,
):
    pairs = [(wigner_far, wigner), (bins_far, bins), (atoms_far, atoms), (node_far, node)]
    copies = [pltpu.make_async_copy(far, near, sems.at[index]) for index, (far, near) in enumerate(pairs)]
    for copy in copies:
        copy.start()
    for copy in copies[0:3]:
        copy.wait()
    load_frames(frames, padded, wigner, packed_row(bins[...]))
    copies[3].wait()
    row = packed_row(atoms[...])
    wide = 2 * LANES
    group = (iota((GROUPS * LANES, wide), 1) & (LANES - 1)) >> 5
    entry = iota((GROUPS * LANES, wide), 0)
    table = jnp.where(entry == row + group * LANES, 1.0, 0.0).astype(f32).astype(bf16)
    left = jnp.concatenate(
        [flat(node[:, g * SUB : (g + 1) * SUB, :]) for g in range(GROUPS)], axis=1
    )
    gathered[...] = dot(left, table).reshape(COEF, SUB, wide)
    rotate_into(frames, gathered, rotated, SUB)
    outer[...] = rotated[:, :, pl.ds(pl.multiple_of(core[0] * LANES, LANES), LANES)]
    inner[...] = rotated[:, :, pl.ds(pl.multiple_of((1 - core[0]) * LANES, LANES), LANES)]


def pre_kernel(node, wigner, sources, bins, inner_in, rotated, inner, frames, padded, values):
    load_frames(frames, padded, wigner, bins[...])
    values[...] = dot(flat(node[...]), one_hot(sources[...])).reshape(COEF, CH, LANES)
    rotate_into(frames, values, rotated, CH)
    inner[...] = inner_in[...]


def cot_kernel(cot, wigner, targets, bins, halo_targets, halo_bins, after, message_grad, frames, padded, values):
    joint_bins = jnp.concatenate([bins[...], halo_row(halo_bins[...], -1)], axis=1)
    joint_targets = jnp.concatenate([targets[...], halo_row(halo_targets[...], -1)], axis=1)
    load_frames(frames, padded, wigner, joint_bins)
    table = one_hot(joint_targets, 0.5)
    for part in (slice(0, LANES), slice(LANES, WIDE)):
        values[:, :, part] = dot(flat(cot[...]), table[:, part]).reshape(COEF, CH, LANES)
        rotate_into(frames.at[:, :, part], values.at[:, :, part], message_grad.at[:, :, part], CH)


def rows_of(values, first, last):
    return flat(values[first[0] // CH : last[1] // CH])


def conv_forward(rotated, conv, w_zero, w_one, w_two):
    def put(span, value):
        conv[span[0] // CH : span[1] // CH] = value.reshape(-1, CH, WIDE)

    put(ZERO, dot(w_zero[...], rows_of(rotated, ZERO, ZERO)))
    both = rows_of(rotated, PLUS1, MINUS1)
    put(PLUS1, dot(jnp.concatenate([w_one[0], -w_one[1]], axis=1), both))
    put(MINUS1, dot(jnp.concatenate([w_one[1], w_one[0]], axis=1), both))
    plus, minus = rows_of(rotated, PLUS2, PLUS2), rows_of(rotated, MINUS2, MINUS2)
    put(PLUS2, dot(w_two[0], plus) - dot(w_two[1], minus))
    put(MINUS2, dot(w_two[1], plus) + dot(w_two[0], minus))


def spread_table():
    shape = (2 * LANES, GROUPS * LANES)
    lane, column = iota(shape, 0), iota(shape, 1)
    slot, where = lane >> 7, lane & (LANES - 1)
    group, inside = column >> 7, column & (LANES - 1)
    same = (where >> 5 == group) & (inside == slot * CAP + (where & (CAP - 1)))
    return jnp.where(same, 1.0, 0.0).astype(f32).astype(bf16)


def pack_grads(packed, values):
    at = 0
    for value in values:
        height, width = value.shape
        for first in range(0, width - LANES + 1, LANES):
            packed[at : at + height, :] = value[:, first : first + LANES].astype(bf16)
            at += height
        if width % LANES:
            first, half = width - width % LANES, height // 2
            piece = value[:, first:width]
            packed[at : at + half, :] = jnp.concatenate([piece[0:half], piece[half:]], axis=1).astype(bf16)
            at += half
    packed[at:, :] = jnp.zeros((packed.shape[0] - at, LANES), bf16)


def conv_kernel(
    core, outer, inner, inner_rotated, message_grad, w_zero, w_one, w_two, scale, halo_scale,
    conv_grad, message, keep, send,
    rotated, conv, packed, halo,
):
    rotated[:, :, 0:LANES] = inner_rotated[...]
    halo[core[0]] = flat(outer[...])
    halo[1 - core[0]] = flat(inner[...])
    left = jnp.concatenate([halo[0], halo[1]], axis=1)
    spread = dot(left, spread_table()).astype(bf16)
    for g in range(GROUPS):
        rotated[:, g * SUB : (g + 1) * SUB, LANES:WIDE] = spread[:, g * LANES : (g + 1) * LANES].reshape(
            TRUNC, SUB, LANES
        )
    conv_forward(rotated, conv, w_zero, w_one, w_two)
    weight = jnp.concatenate([scale[...], halo_row(halo_scale[...], 0.0)], axis=1)
    gating = jax.nn.sigmoid(conv[0])
    factor = gating * weight
    factor_grad = message_grad[0] * conv[0]
    for row in range(1, TRUNC):
        value = conv[row]
        grad = message_grad[row]
        factor_grad = factor_grad + grad * value
        conv_grad[row] = (grad * factor).astype(bf16)
        message[row] = value * factor
    conv_grad[0] = (message_grad[0] * factor + factor_grad * weight * gating * (1.0 - gating)).astype(bf16)
    message[0] = conv[0] * factor

    zero = dot_nt(rows_of(conv_grad, ZERO, ZERO), rows_of(rotated, ZERO, ZERO))
    pairs = []
    for plus, minus in ((PLUS1, MINUS1), (PLUS2, MINUS2)):
        g_plus, g_minus = rows_of(conv_grad, plus, plus), rows_of(conv_grad, minus, minus)
        inputs = jnp.concatenate([rows_of(rotated, plus, plus), rows_of(rotated, minus, minus)], axis=1)
        pairs.append([
            dot_nt(jnp.concatenate([g_plus, g_minus], axis=1), inputs),
            dot_nt(jnp.concatenate([g_minus, -g_plus], axis=1), inputs),
        ])
    one, two = pairs
    pack_grads(packed.at[0], [zero, one[0]])
    pack_grads(packed.at[1], [one[1]] + two)
    keep[...] = packed[core[0]]
    send[...] = packed[1 - core[0]]


def input_kernel(conv_grad, w_zero, w_one, w_two, after, to_lower, to_upper, inner, joint):
    def put(span, value):
        joint[span[0] // CH : span[1] // CH] = value.astype(bf16).reshape(-1, CH, WIDE)

    put(ZERO, dot_tn(w_zero[...], rows_of(conv_grad, ZERO, ZERO)))
    for weights, plus, minus in ((w_one, PLUS1, MINUS1), (w_two, PLUS2, MINUS2)):
        both = flat(weights[...])
        put(plus, dot_tn(both, rows_of(conv_grad, plus, minus)))
        crossed = jnp.concatenate([rows_of(conv_grad, minus, minus), -rows_of(conv_grad, plus, plus)], axis=0)
        put(minus, dot_tn(both, crossed))
    left = jnp.concatenate(
        [flat(joint[:, g * SUB : (g + 1) * SUB, LANES:WIDE]) for g in range(GROUPS)], axis=1
    )
    shape = (GROUPS * LANES, WIDE)
    column, lane = iota(shape, 0), iota(shape, 1)
    slot, where = lane >> 7, lane & (LANES - 1)
    group, inside = column >> 7, column & (LANES - 1)
    same = (where >> 5 == group) & (inside == slot * CAP + (where & (CAP - 1)))
    gathered = dot(left, jnp.where(same, 1.0, 0.0).astype(f32).astype(bf16)).astype(bf16)
    to_lower[...] = gathered[:, 0:LANES].reshape(TRUNC, SUB, LANES)
    to_upper[...] = gathered[:, LANES:WIDE].reshape(TRUNC, SUB, LANES)
    inner[...] = joint[:, :, 0:LANES]


def update_kernel(
    node, wigner, message, bins, targets, halo_bins, halo_targets, after,
    updated, token, frames, padded, part,
):
    joint_bins = jnp.concatenate([bins[...], halo_row(halo_bins[...], -1)], axis=1)
    joint_targets = jnp.concatenate([targets[...], halo_row(halo_targets[...], -1)], axis=1)
    load_frames(frames, padded, wigner, joint_bins)
    rotate_back(frames, message, part, 16)
    summed = dot_nt(flat(part[...]), one_hot(joint_targets, 0.5)).reshape(COEF, CH, LANES)
    updated[...] = (node[...].astype(f32) + summed).astype(bf16)
    token[...] = jnp.zeros(token.shape, token.dtype)


def back_kernel(
    back_zero, back_one, inner, wigner, rim_bins, atoms, bins, sources, cot, after, feature_grad, token,
    frames, inner_frames, padded, joint, rim_grad, inner_grad,
):
    load_frames(inner_frames, padded, wigner, bins[...])
    rotate_back(inner_frames, inner, inner_grad, 32)
    load_frames(frames, padded, wigner, packed_row(rim_bins[...]))
    joint[:, :, 0:LANES] = back_zero[...]
    joint[:, :, LANES:WIDE] = back_one[...]
    rotate_back(frames, joint, rim_grad, SUB)
    row = packed_row(atoms[...])
    group = (iota((LANES, WIDE), 1) & (LANES - 1)) >> 5
    entry = iota((LANES, WIDE), 0)
    values = flat(rim_grad[...])
    inner_table = one_hot(sources[...])
    for g in range(GROUPS):
        part = slice(g * SUB, (g + 1) * SUB)
        table = jnp.where((entry == row) & (group == g), 1.0, 0.0).astype(f32).astype(bf16)
        scattered = dot_nt(values, table) + dot_nt(flat(inner_grad[:, part, :]), inner_table)
        feature_grad[:, part, :] = cot[:, part, :].astype(f32) + scattered.reshape(COEF, SUB, LANES)
    token[...] = jnp.zeros(token.shape, token.dtype)


def add_kernel(pieces, after, total):
    found = pieces[0].astype(f32)
    for index in range(1, pieces.shape[0]):
        found = found + pieces[index].astype(f32)
    found = found.astype(bf16)
    if total.ndim == 2:
        total[...] = found
    else:
        for index in range(total.shape[0]):
            total[index] = found


def leave_kernel(conv_grad, message, conv_grad_far, message_far, token, sems):
    puts = [
        pltpu.make_async_copy(conv_grad, conv_grad_far, sems.at[0]),
        pltpu.make_async_copy(message, message_far, sems.at[1]),
    ]
    for put in puts:
        put.start()
    token[...] = jnp.zeros(token.shape, token.dtype)
    for put in puts:
        put.wait()


def join_kernel(keep, other, after, joint_far, joint, sems):
    count = sems.shape[0]
    rows = joint.shape[0] // count
    copies = []
    for index in range(count):
        part = slice(index * rows, (index + 1) * rows)
        joint[part, :] = (keep[part, :].astype(f32) + other[part, :].astype(f32)).astype(bf16)
        copies.append(pltpu.make_async_copy(joint.at[part, :], joint_far.at[part, :], sems.at[index]))
        copies[-1].start()
    for copy in copies:
        copy.wait()


def unpack_kernel(replicas, swapped, which, packed, *refs):
    (zero, one, two), (zero_v, one_v, two_v), sems = refs[-7:-4], refs[-4:-1], refs[-1]

    def write(pairs):
        at = 0
        copies = []
        for index, (ref, out) in enumerate(pairs):
            height, width = ref.shape
            for first in range(0, width - LANES + 1, LANES):
                ref[:, first : first + LANES] = packed[at : at + height, :].astype(f32) * (1.0 / replicas)
                at += height
            if width % LANES:
                first, part = width - width % LANES, height // 2
                value = packed[at : at + part, :].astype(f32) * (1.0 / replicas)
                ref[0:part, first:width] = value[:, 0 : width - first]
                ref[part:height, first:width] = value[:, width - first :]
                at += part
            copy = pltpu.make_async_copy(ref, out, sems.at[index])
            copy.start()
            copies.append(copy)
        for copy in copies:
            copy.wait()

    half = 1 - which[0] if swapped else which[0]

    @pl.when(half == 0)
    def first():
        write([(zero_v, zero), (one_v.at[0], one.at[0])])

    @pl.when(half == 1)
    def second():
        write([(one_v.at[1], one.at[1]), (two_v.at[0], two.at[0]), (two_v.at[1], two.at[1])])


def call(kernel, outs, scratch, operands, flops, name, scalars=0, far=0, hbm=0, far_outs=0, aliases=None):
    whole = pl.BlockSpec(memory_space=pltpu.VMEM)
    scalar = pl.BlockSpec(memory_space=pltpu.SMEM)
    away = pl.BlockSpec(memory_space=pl.ANY)
    main = pl.BlockSpec(memory_space=pltpu.HBM)
    moved = sum(v.size * v.dtype.itemsize for v in list(operands) + list(outs))
    operands = list(operands)
    for index in range(len(operands) - hbm, len(operands)):
        operands[index] = pltpu.with_memory_space_constraint(operands[index], pltpu.HBM)
    outs = [pltpu.HBM(v.shape, v.dtype) if index < far_outs else v for index, v in enumerate(outs)]
    near = len(operands) - scalars - far - hbm
    return pl.pallas_call(
        kernel,
        out_shape=tuple(outs),
        in_specs=[scalar] * scalars + [whole] * near + [away] * far + [main] * hbm,
        out_specs=tuple([main] * far_outs + [whole] * (len(outs) - far_outs)),
        scratch_shapes=scratch,
        input_output_aliases=aliases or {},
        compiler_params=pltpu.CompilerParams(vmem_limit_bytes=VMEM),
        cost_estimate=pl.CostEstimate(flops=flops, bytes_accessed=moved, transcendentals=0),
        name=name,
    )(*operands)


def arr(shape, dtype):
    return jax.ShapeDtypeStruct(shape, dtype)


def scr(shape, dtype):
    return pltpu.VMEM(shape, dtype)


def from_behind(value, axis, steps):
    count = lax.axis_size(axis)
    return lax.ppermute(value, axis, [(source, (source + steps) % count) for source in range(count)])


def across_chips(value):
    chips = lax.axis_size("z")
    pairs = []
    for chip in range(chips):
        pairs += [(2 * chip, (2 * chip - 1) % (2 * chips)), (2 * chip + 1, (2 * chip + 2) % (2 * chips))]
    return lax.ppermute(value, ("z", "core"), pairs)


def swap_cores(value):
    return lax.ppermute(value, "core", [(0, 1), (1, 0)])


def to_all(copies, axes):
    return lax.all_to_all(copies, axes, 0, 0)


PACKED = 5632
SPLIT = (2, 4, 8)
PLANE = ("x", "y")


def body(
    node_features, cotangent, wigner, w_zero, w_one, w_two, edge_source, edge_target, edge_bin, edge_scale,
    send_atoms, send_bins, recv_targets, recv_bins, recv_scale,
):
    node, cot = node_features[0], cotangent[0]
    table = jnp.transpose(wigner, (2, 1, 0))
    graph = ("z", "core")
    out_atoms, out_bins = send_atoms[0], send_bins[0]
    in_targets, in_bins, in_scale = recv_targets[0], recv_bins[0], recv_scale[0]
    weights = [w_zero, w_one, w_two]
    packed_shape = arr((TRUNC, SUB, LANES), bf16)
    edges16, edges32 = arr((TRUNC, CH, WIDE), bf16), arr((TRUNC, CH, WIDE), f32)
    frames1, frames2 = scr((COEF, PAD_ROWS, LANES), f32), scr((COEF, PAD_ROWS, WIDE), f32)
    padded = scr((COEF, PAD_ROWS, LANES), bf16)
    mark = arr((8, LANES), f32)

    core = lax.axis_index("core").reshape(1)
    outer, inner, near_node, near_table = call(
        rim_kernel, [packed_shape] * 2 + [arr(node.shape, bf16), arr(table.shape, bf16)],
        [frames2, padded, scr((COEF, SUB, WIDE), f32), scr((TRUNC, SUB, WIDE), bf16),
         scr(out_atoms.shape, jnp.int32),
         scr(out_bins.shape, jnp.int32), pltpu.SemaphoreType.DMA((4,))],
        [core, node, table, out_atoms, out_bins], 10**9, "rim", scalars=1, hbm=4,
    )
    outer = across_chips(outer)
    inner_rotated, inner = call(
        pre_kernel, [arr((TRUNC, CH, LANES), bf16), packed_shape],
        [frames1, padded, scr((COEF, CH, LANES), f32)],
        [near_node, near_table, edge_source, edge_bin, inner], 10**10, "pre",
    )
    (message_grad,) = call(
        cot_kernel, [edges32], [frames2, padded, scr((COEF, CH, WIDE), f32)],
        [cot, near_table, edge_target, edge_bin, in_targets, in_bins, inner], 10**10, "cotangent", far=1,
    )
    inner = swap_cores(inner)
    half = arr((PACKED // 2, LANES), bf16)
    conv_grad, message, keep, send = call(
        conv_kernel, [edges16, edges32, half, half],
        [scr((TRUNC, CH, WIDE), bf16), scr((TRUNC, CH, WIDE), f32), scr((2, PACKED // 2, LANES), bf16),
         scr((2, TRUNC * SUB, LANES), bf16)],
        [core, outer, inner, inner_rotated, message_grad] + weights + [edge_scale, in_scale],
        10**10, "conv", scalars=1,
    )

    pieces = lax.axis_size(PLANE)
    other = swap_cores(send)
    conv_grad, message, token = call(
        leave_kernel, [edges16, edges32, mark], [pltpu.SemaphoreType.DMA((2,))], [conv_grad, message], 10**6, "leave",
        far_outs=2,
    )
    (joint,) = call(
        join_kernel, [half], [scr(half.shape, bf16), pltpu.SemaphoreType.DMA((4,))], [keep, other, token],
        10**6, "join", far=1, far_outs=1,
    )
    joint = joint.reshape(pieces, -1, LANES)
    piece = joint.shape[1:]
    parts = to_all(joint, PLANE)
    back_lower, back_upper, inner = call(
        input_kernel, [packed_shape, packed_shape, arr((TRUNC, CH, LANES), bf16)], [scr((TRUNC, CH, WIDE), bf16)],
        [conv_grad] + weights + [joint], 10**10, "inputs", far=1,
    )
    back_zero = from_behind(back_upper, graph, 1)
    back_one = from_behind(back_lower, graph, -1)
    updated, token = call(
        update_kernel, [arr((COEF, CH, LANES), bf16), mark],
        [frames2, padded, scr((COEF, CH, WIDE), bf16)],
        [node, table, message, edge_bin, edge_target, in_bins, in_targets, inner], 10**10, "update", far=1,
    )
    feature_grad, token = call(
        back_kernel, [arr((COEF, CH, LANES), f32), mark],
        [frames2, frames1, padded, scr((TRUNC, SUB, WIDE), bf16), scr((COEF, SUB, WIDE), bf16),
         scr((COEF, CH, LANES), bf16)],
        [back_zero, back_one, inner, table, out_bins, out_atoms, edge_bin, edge_source, cot, token], 10**10,
        "back", far=1,
    )
    layers = lax.axis_size("z")
    (copies,) = call(add_kernel, [arr((layers,) + piece, bf16)], [], [parts, token], 10**7, "add_plane", far=1)
    sums = to_all(copies, "z")
    (copies,) = call(add_kernel, [arr((pieces,) + piece, bf16)], [], [sums, token], 10**7, "add_z", far=1)
    mine = to_all(copies, PLANE)
    other = swap_cores(mine)
    grads = []
    for swapped, value in enumerate((mine, other)):
        grads = call(
            functools.partial(unpack_kernel, pieces, swapped), [arr(w.shape, f32) for w in weights],
            [scr(w.shape, f32) for w in weights] + [pltpu.SemaphoreType.DMA((3,))],
            [core, value.reshape(half.shape)] + list(grads), 10**7, "unpack", scalars=1, hbm=len(grads),
            far_outs=3, aliases={2 + index: index for index in range(len(grads))},
        )
    grad_zero, grad_one, grad_two = grads
    return updated[None], feature_grad[None], grad_zero, grad_one, grad_two


def solution(mesh):
    cores, rows, columns = SPLIT
    graph = mesh.shape["graph"]
    fine = jax.sharding.Mesh(mesh.devices.reshape(graph // cores, cores, rows, columns), ("z", "core", "x", "y"))
    dp, along = PLANE, ("z", "core")
    nodes, edges = P(dp, None, None, along), P(dp, along)
    in_specs = (nodes, nodes) + (P(),) * 4 + (edges,) * 4 + (P(dp, along, None),) * 5
    return jax.shard_map(
        body, mesh=fine, in_specs=in_specs, out_specs=(nodes, nodes, P(), P(), P()), check_vma=False
    )
```

```python
import functools

import jax
import jax.numpy as jnp
from jax import lax
from jax.experimental import pallas as pl
from jax.experimental.pallas import tpu as pltpu
from jax.sharding import PartitionSpec as P

COEF, TRUNC, CH, LANES = 49, 29, 64, 128
CAP, GROUPS, SUB = 32, 4, 16
WIDE = 2 * LANES
PAD_ROWS = 32
ZERO, PLUS1, MINUS1, PLUS2, MINUS2 = (0, 448), (448, 832), (832, 1216), (1216, 1536), (1536, 1856)
VMEM = 24 * 1024 * 1024
f32, bf16 = jnp.float32, jnp.bfloat16


def degree_rows(degree):
    rows = [degree]
    if degree >= 1:
        rows = rows + [6 + degree, 12 + degree]
    if degree >= 2:
        rows = rows + [17 + degree, 22 + degree]
    return rows


def dot(left, right):
    return jnp.dot(left, right, preferred_element_type=f32)


def dot_nt(left, right):
    return lax.dot_general(left, right, (((1,), (1,)), ((), ())), preferred_element_type=f32)


def dot_tn(left, right):
    return lax.dot_general(left, right, (((0,), (0,)), ((), ())), preferred_element_type=f32)


def iota(shape, axis):
    return lax.broadcasted_iota(jnp.int32, shape, axis)


def one_hot(index, value=1.0):
    lanes = index.shape[1]
    return jnp.where(iota((LANES, lanes), 0) == index, value, 0.0).astype(f32).astype(bf16)


def load_frames(frames, padded, wigner, bins):
    padded[:, 0:TRUNC, :] = wigner[...]
    lanes = bins.shape[1]
    found = dot(padded[...].reshape(COEF * PAD_ROWS, LANES), one_hot(bins))
    frames[...] = found.reshape(COEF, PAD_ROWS, lanes)


def rotate_into(frames, values, found, chunk):
    channels = values.shape[1]

    def step(index, carry):
        part = pl.ds(pl.multiple_of(index * chunk, chunk), chunk)
        for degree in range(7):
            rows = degree_rows(degree)
            total = {}
            for k in range(degree * degree, (degree + 1) * (degree + 1)):
                value = values[k, part, :].astype(f32)
                for row in rows:
                    term = frames[k, row : row + 1, :] * value
                    total[row] = term if row not in total else total[row] + term
            for row in rows:
                found[row, part, :] = total[row].astype(found.dtype)
        return carry

    lax.fori_loop(0, channels // chunk, step, 0)


def rotate_back(frames, values, found, chunk):
    channels = values.shape[1]

    def step(index, carry):
        part = pl.ds(pl.multiple_of(index * chunk, chunk), chunk)
        for degree in range(7):
            rows = degree_rows(degree)
            held = {row: values[row, part, :].astype(f32) for row in rows}
            for k in range(degree * degree, (degree + 1) * (degree + 1)):
                total = None
                for row in rows:
                    term = frames[k, row : row + 1, :] * held[row]
                    total = term if total is None else total + term
                found[k, part, :] = total.astype(found.dtype)
        return carry

    lax.fori_loop(0, channels // chunk, step, 0)


def flat(value):
    return value.reshape(value.shape[0] * value.shape[1], value.shape[2])


def halo_row(pair, fill):
    rest = jnp.full((1, LANES - 2 * CAP), fill, pair.dtype)
    return jnp.concatenate([pair[0:1, :], pair[1:2, :], rest], axis=1)


def packed_row(pair):
    pieces = [pair[slot : slot + 1, :] for slot in range(2) for _ in range(GROUPS)]
    return jnp.concatenate(pieces, axis=1)


def rim_kernel(
    core, node_far, wigner_far, atoms_far, bins_far, to_lower, to_upper, node, wigner,
    frames, padded, gathered, rotated, atoms, bins, sems,
):
    pairs = [(wigner_far, wigner), (bins_far, bins), (atoms_far, atoms), (node_far, node)]
    copies = [pltpu.make_async_copy(far, near, sems.at[index]) for index, (far, near) in enumerate(pairs)]
    for copy in copies:
        copy.start()
    for copy in copies[0:3]:
        copy.wait()
    load_frames(frames, padded, wigner, packed_row(bins[...]))
    copies[3].wait()
    row = packed_row(atoms[...])
    wide = 2 * LANES
    group = (iota((GROUPS * LANES, wide), 1) & (LANES - 1)) >> 5
    entry = iota((GROUPS * LANES, wide), 0)
    table = jnp.where(entry == row + group * LANES, 1.0, 0.0).astype(f32).astype(bf16)
    left = jnp.concatenate(
        [flat(node[:, g * SUB : (g + 1) * SUB, :]) for g in range(GROUPS)], axis=1
    )
    gathered[...] = dot(left, table).reshape(COEF, SUB, wide)
    rotate_into(frames, gathered, rotated, SUB)
    to_lower[...] = rotated[:, :, 0:LANES]
    to_upper[...] = rotated[:, :, LANES:wide]


def pre_kernel(
    node, cot, wigner, sources, targets, bins, halo_targets, halo_bins,
    rotated, message_grad, frames, padded, values,
):
    joint_bins = jnp.concatenate([bins[...], halo_row(halo_bins[...], -1)], axis=1)
    joint_targets = jnp.concatenate([targets[...], halo_row(halo_targets[...], -1)], axis=1)
    load_frames(frames, padded, wigner, joint_bins)
    inner, halo = slice(0, LANES), slice(LANES, WIDE)
    values[:, :, inner] = dot(flat(node[...]), one_hot(sources[...])).reshape(COEF, CH, LANES)
    rotate_into(frames.at[:, :, inner], values.at[:, :, inner], rotated, CH)
    table = one_hot(joint_targets, 0.5)
    for part in (inner, halo):
        values[:, :, part] = dot(flat(cot[...]), table[:, part]).reshape(COEF, CH, LANES)
        rotate_into(frames.at[:, :, part], values.at[:, :, part], message_grad.at[:, :, part], CH)


def rows_of(values, first, last):
    return flat(values[first[0] // CH : last[1] // CH])


def conv_forward(rotated, conv, w_zero, w_one, w_two):
    def put(span, value):
        conv[span[0] // CH : span[1] // CH] = value.reshape(-1, CH, WIDE)

    put(ZERO, dot(w_zero[...], rows_of(rotated, ZERO, ZERO)))
    both = rows_of(rotated, PLUS1, MINUS1)
    put(PLUS1, dot(jnp.concatenate([w_one[0], -w_one[1]], axis=1), both))
    put(MINUS1, dot(jnp.concatenate([w_one[1], w_one[0]], axis=1), both))
    plus, minus = rows_of(rotated, PLUS2, PLUS2), rows_of(rotated, MINUS2, MINUS2)
    put(PLUS2, dot(w_two[0], plus) - dot(w_two[1], minus))
    put(MINUS2, dot(w_two[1], plus) + dot(w_two[0], minus))


def spread_table():
    shape = (2 * LANES, GROUPS * LANES)
    lane, column = iota(shape, 0), iota(shape, 1)
    slot, where = lane >> 7, lane & (LANES - 1)
    group, inside = column >> 7, column & (LANES - 1)
    same = (where >> 5 == group) & (inside == slot * CAP + (where & (CAP - 1)))
    return jnp.where(same, 1.0, 0.0).astype(f32).astype(bf16)


def pack_grads(packed, values):
    at = 0
    for value in values:
        height, width = value.shape
        for first in range(0, width - LANES + 1, LANES):
            packed[at : at + height, :] = value[:, first : first + LANES].astype(bf16)
            at += height
        if width % LANES:
            first, half = width - width % LANES, height // 2
            piece = value[:, first:width]
            packed[at : at + half, :] = jnp.concatenate([piece[0:half], piece[half:]], axis=1).astype(bf16)
            at += half
    packed[at:, :] = jnp.zeros((packed.shape[0] - at, LANES), bf16)


def conv_kernel(
    core, from_lower, from_upper, inner_rotated, message_grad, w_zero, w_one, w_two, scale, halo_scale,
    conv_grad, message, keep, send,
    rotated, conv, packed,
):
    rotated[:, :, 0:LANES] = inner_rotated[...]
    left = jnp.concatenate([flat(from_lower[...]), flat(from_upper[...])], axis=1)
    spread = dot(left, spread_table()).astype(bf16)
    for g in range(GROUPS):
        rotated[:, g * SUB : (g + 1) * SUB, LANES:WIDE] = spread[:, g * LANES : (g + 1) * LANES].reshape(
            TRUNC, SUB, LANES
        )
    conv_forward(rotated, conv, w_zero, w_one, w_two)
    weight = jnp.concatenate([scale[...], halo_row(halo_scale[...], 0.0)], axis=1)
    gating = jax.nn.sigmoid(conv[0])
    factor = gating * weight
    factor_grad = message_grad[0] * conv[0]
    for row in range(1, TRUNC):
        value = conv[row]
        grad = message_grad[row]
        factor_grad = factor_grad + grad * value
        conv_grad[row] = (grad * factor).astype(bf16)
        message[row] = value * factor
    conv_grad[0] = (message_grad[0] * factor + factor_grad * weight * gating * (1.0 - gating)).astype(bf16)
    message[0] = conv[0] * factor

    zero = dot_nt(rows_of(conv_grad, ZERO, ZERO), rows_of(rotated, ZERO, ZERO))
    pairs = []
    for plus, minus in ((PLUS1, MINUS1), (PLUS2, MINUS2)):
        g_plus, g_minus = rows_of(conv_grad, plus, plus), rows_of(conv_grad, minus, minus)
        inputs = jnp.concatenate([rows_of(rotated, plus, plus), rows_of(rotated, minus, minus)], axis=1)
        pairs.append([
            dot_nt(jnp.concatenate([g_plus, g_minus], axis=1), inputs),
            dot_nt(jnp.concatenate([g_minus, -g_plus], axis=1), inputs),
        ])
    one, two = pairs
    pack_grads(packed.at[0], [zero, one[0]])
    pack_grads(packed.at[1], [one[1]] + two)
    keep[...] = packed[core[0]]
    send[...] = packed[1 - core[0]]


def input_kernel(conv_grad, w_zero, w_one, w_two, after, to_lower, to_upper, inner, joint):
    def put(span, value):
        joint[span[0] // CH : span[1] // CH] = value.astype(bf16).reshape(-1, CH, WIDE)

    put(ZERO, dot_tn(w_zero[...], rows_of(conv_grad, ZERO, ZERO)))
    for weights, plus, minus in ((w_one, PLUS1, MINUS1), (w_two, PLUS2, MINUS2)):
        both = flat(weights[...])
        put(plus, dot_tn(both, rows_of(conv_grad, plus, minus)))
        crossed = jnp.concatenate([rows_of(conv_grad, minus, minus), -rows_of(conv_grad, plus, plus)], axis=0)
        put(minus, dot_tn(both, crossed))
    left = jnp.concatenate(
        [flat(joint[:, g * SUB : (g + 1) * SUB, LANES:WIDE]) for g in range(GROUPS)], axis=1
    )
    shape = (GROUPS * LANES, WIDE)
    column, lane = iota(shape, 0), iota(shape, 1)
    slot, where = lane >> 7, lane & (LANES - 1)
    group, inside = column >> 7, column & (LANES - 1)
    same = (where >> 5 == group) & (inside == slot * CAP + (where & (CAP - 1)))
    gathered = dot(left, jnp.where(same, 1.0, 0.0).astype(f32).astype(bf16)).astype(bf16)
    to_lower[...] = gathered[:, 0:LANES].reshape(TRUNC, SUB, LANES)
    to_upper[...] = gathered[:, LANES:WIDE].reshape(TRUNC, SUB, LANES)
    inner[...] = joint[:, :, 0:LANES]


def update_kernel(
    node, wigner, message, bins, targets, halo_bins, halo_targets, after,
    updated, token, frames, padded, part,
):
    joint_bins = jnp.concatenate([bins[...], halo_row(halo_bins[...], -1)], axis=1)
    joint_targets = jnp.concatenate([targets[...], halo_row(halo_targets[...], -1)], axis=1)
    load_frames(frames, padded, wigner, joint_bins)
    rotate_back(frames, message, part, 16)
    summed = dot_nt(flat(part[...]), one_hot(joint_targets, 0.5)).reshape(COEF, CH, LANES)
    updated[...] = (node[...].astype(f32) + summed).astype(bf16)
    token[...] = jnp.zeros(token.shape, token.dtype)


def back_kernel(
    back_zero, back_one, inner, wigner, rim_bins, atoms, bins, sources, cot, after, feature_grad, token,
    frames, inner_frames, padded, joint, rim_grad, inner_grad,
):
    load_frames(inner_frames, padded, wigner, bins[...])
    rotate_back(inner_frames, inner, inner_grad, 32)
    load_frames(frames, padded, wigner, packed_row(rim_bins[...]))
    joint[:, :, 0:LANES] = back_zero[...]
    joint[:, :, LANES:WIDE] = back_one[...]
    rotate_back(frames, joint, rim_grad, SUB)
    row = packed_row(atoms[...])
    group = (iota((LANES, WIDE), 1) & (LANES - 1)) >> 5
    entry = iota((LANES, WIDE), 0)
    values = flat(rim_grad[...])
    inner_table = one_hot(sources[...])
    for g in range(GROUPS):
        part = slice(g * SUB, (g + 1) * SUB)
        table = jnp.where((entry == row) & (group == g), 1.0, 0.0).astype(f32).astype(bf16)
        scattered = dot_nt(values, table) + dot_nt(flat(inner_grad[:, part, :]), inner_table)
        feature_grad[:, part, :] = cot[:, part, :].astype(f32) + scattered.reshape(COEF, SUB, LANES)
    token[...] = jnp.zeros(token.shape, token.dtype)


def add_kernel(pieces, after, total):
    found = pieces[0].astype(f32)
    for index in range(1, pieces.shape[0]):
        found = found + pieces[index].astype(f32)
    found = found.astype(bf16)
    if total.ndim == 2:
        total[...] = found
    else:
        for index in range(total.shape[0]):
            total[index] = found


def leave_kernel(conv_grad, message, conv_grad_far, message_far, token, sems):
    puts = [
        pltpu.make_async_copy(conv_grad, conv_grad_far, sems.at[0]),
        pltpu.make_async_copy(message, message_far, sems.at[1]),
    ]
    for put in puts:
        put.start()
    token[...] = jnp.zeros(token.shape, token.dtype)
    for put in puts:
        put.wait()


def join_kernel(keep, other, after, joint_far, joint, sems):
    count = sems.shape[0]
    rows = joint.shape[0] // count
    copies = []
    for index in range(count):
        part = slice(index * rows, (index + 1) * rows)
        joint[part, :] = (keep[part, :].astype(f32) + other[part, :].astype(f32)).astype(bf16)
        copies.append(pltpu.make_async_copy(joint.at[part, :], joint_far.at[part, :], sems.at[index]))
        copies[-1].start()
    for copy in copies:
        copy.wait()


def unpack_kernel(replicas, swapped, which, packed, *refs):
    (zero, one, two), (zero_v, one_v, two_v), sems = refs[-7:-4], refs[-4:-1], refs[-1]

    def write(pairs):
        at = 0
        copies = []
        for index, (ref, out) in enumerate(pairs):
            height, width = ref.shape
            for first in range(0, width - LANES + 1, LANES):
                ref[:, first : first + LANES] = packed[at : at + height, :].astype(f32) * (1.0 / replicas)
                at += height
            if width % LANES:
                first, part = width - width % LANES, height // 2
                value = packed[at : at + part, :].astype(f32) * (1.0 / replicas)
                ref[0:part, first:width] = value[:, 0 : width - first]
                ref[part:height, first:width] = value[:, width - first :]
                at += part
            copy = pltpu.make_async_copy(ref, out, sems.at[index])
            copy.start()
            copies.append(copy)
        for copy in copies:
            copy.wait()

    half = 1 - which[0] if swapped else which[0]

    @pl.when(half == 0)
    def first():
        write([(zero_v, zero), (one_v.at[0], one.at[0])])

    @pl.when(half == 1)
    def second():
        write([(one_v.at[1], one.at[1]), (two_v.at[0], two.at[0]), (two_v.at[1], two.at[1])])


def call(kernel, outs, scratch, operands, flops, name, scalars=0, far=0, hbm=0, far_outs=0, aliases=None):
    whole = pl.BlockSpec(memory_space=pltpu.VMEM)
    scalar = pl.BlockSpec(memory_space=pltpu.SMEM)
    away = pl.BlockSpec(memory_space=pl.ANY)
    main = pl.BlockSpec(memory_space=pltpu.HBM)
    moved = sum(v.size * v.dtype.itemsize for v in list(operands) + list(outs))
    operands = list(operands)
    for index in range(len(operands) - hbm, len(operands)):
        operands[index] = pltpu.with_memory_space_constraint(operands[index], pltpu.HBM)
    outs = [pltpu.HBM(v.shape, v.dtype) if index < far_outs else v for index, v in enumerate(outs)]
    near = len(operands) - scalars - far - hbm
    return pl.pallas_call(
        kernel,
        out_shape=tuple(outs),
        in_specs=[scalar] * scalars + [whole] * near + [away] * far + [main] * hbm,
        out_specs=tuple([main] * far_outs + [whole] * (len(outs) - far_outs)),
        scratch_shapes=scratch,
        input_output_aliases=aliases or {},
        compiler_params=pltpu.CompilerParams(vmem_limit_bytes=VMEM),
        cost_estimate=pl.CostEstimate(flops=flops, bytes_accessed=moved, transcendentals=0),
        name=name,
    )(*operands)


def arr(shape, dtype):
    return jax.ShapeDtypeStruct(shape, dtype)


def scr(shape, dtype):
    return pltpu.VMEM(shape, dtype)


def from_behind(value, axis, steps):
    count = lax.axis_size(axis)
    return lax.ppermute(value, axis, [(source, (source + steps) % count) for source in range(count)])


def swap_cores(value):
    return lax.ppermute(value, "core", [(0, 1), (1, 0)])


def to_all(copies, axes):
    return lax.all_to_all(copies, axes, 0, 0)


PACKED = 5632
SPLIT = (2, 4, 8)
PLANE = ("x", "y")


def body(
    node_features, cotangent, wigner, w_zero, w_one, w_two, edge_source, edge_target, edge_bin, edge_scale,
    send_atoms, send_bins, recv_targets, recv_bins, recv_scale,
):
    node, cot = node_features[0], cotangent[0]
    table = jnp.transpose(wigner, (2, 1, 0))
    graph = ("z", "core")
    out_atoms, out_bins = send_atoms[0], send_bins[0]
    in_targets, in_bins, in_scale = recv_targets[0], recv_bins[0], recv_scale[0]
    weights = [w_zero, w_one, w_two]
    packed_shape = arr((TRUNC, SUB, LANES), bf16)
    edges16, edges32 = arr((TRUNC, CH, WIDE), bf16), arr((TRUNC, CH, WIDE), f32)
    frames1, frames2 = scr((COEF, PAD_ROWS, LANES), f32), scr((COEF, PAD_ROWS, WIDE), f32)
    padded = scr((COEF, PAD_ROWS, LANES), bf16)
    mark = arr((8, LANES), f32)

    core = lax.axis_index("core").reshape(1)
    to_lower, to_upper, near_node, near_table = call(
        rim_kernel, [packed_shape] * 2 + [arr(node.shape, bf16), arr(table.shape, bf16)],
        [frames2, padded, scr((COEF, SUB, WIDE), f32), scr((TRUNC, SUB, WIDE), bf16),
         scr(out_atoms.shape, jnp.int32),
         scr(out_bins.shape, jnp.int32), pltpu.SemaphoreType.DMA((4,))],
        [core, node, table, out_atoms, out_bins], 10**9, "rim", scalars=1, hbm=4,
    )
    from_lower = from_behind(to_upper, graph, 1)
    from_upper = from_behind(to_lower, graph, -1)
    inner_rotated, message_grad = call(
        pre_kernel, [arr((TRUNC, CH, LANES), bf16), edges32],
        [frames2, padded, scr((COEF, CH, WIDE), f32)],
        [near_node, cot, near_table, edge_source, edge_target, edge_bin, in_targets, in_bins], 10**10, "pre",
    )
    half = arr((PACKED // 2, LANES), bf16)
    conv_grad, message, keep, send = call(
        conv_kernel, [edges16, edges32, half, half],
        [scr((TRUNC, CH, WIDE), bf16), scr((TRUNC, CH, WIDE), f32), scr((2, PACKED // 2, LANES), bf16)],
        [core, from_lower, from_upper, inner_rotated, message_grad] + weights + [edge_scale, in_scale],
        10**10, "conv", scalars=1,
    )

    pieces = lax.axis_size(PLANE)
    other = swap_cores(send)
    conv_grad, message, token = call(
        leave_kernel, [edges16, edges32, mark], [pltpu.SemaphoreType.DMA((2,))], [conv_grad, message], 10**6, "leave",
        far_outs=2,
    )
    (joint,) = call(
        join_kernel, [half], [scr(half.shape, bf16), pltpu.SemaphoreType.DMA((4,))], [keep, other, token],
        10**6, "join", far=1, far_outs=1,
    )
    joint = joint.reshape(pieces, -1, LANES)
    piece = joint.shape[1:]
    parts = to_all(joint, PLANE)
    back_lower, back_upper, inner = call(
        input_kernel, [packed_shape, packed_shape, arr((TRUNC, CH, LANES), bf16)], [scr((TRUNC, CH, WIDE), bf16)],
        [conv_grad] + weights + [joint], 10**10, "inputs", far=1,
    )
    back_zero = from_behind(back_upper, graph, 1)
    back_one = from_behind(back_lower, graph, -1)
    updated, token = call(
        update_kernel, [arr((COEF, CH, LANES), bf16), mark],
        [frames2, padded, scr((COEF, CH, WIDE), bf16)],
        [node, table, message, edge_bin, edge_target, in_bins, in_targets, inner], 10**10, "update", far=1,
    )
    feature_grad, token = call(
        back_kernel, [arr((COEF, CH, LANES), f32), mark],
        [frames2, frames1, padded, scr((TRUNC, SUB, WIDE), bf16), scr((COEF, SUB, WIDE), bf16),
         scr((COEF, CH, LANES), bf16)],
        [back_zero, back_one, inner, table, out_bins, out_atoms, edge_bin, edge_source, cot, token], 10**10,
        "back", far=1,
    )
    layers = lax.axis_size("z")
    (copies,) = call(add_kernel, [arr((layers,) + piece, bf16)], [], [parts, token], 10**7, "add_plane", far=1)
    sums = to_all(copies, "z")
    (copies,) = call(add_kernel, [arr((pieces,) + piece, bf16)], [], [sums, token], 10**7, "add_z", far=1)
    mine = to_all(copies, PLANE)
    other = swap_cores(mine)
    grads = []
    for swapped, value in enumerate((mine, other)):
        grads = call(
            functools.partial(unpack_kernel, pieces, swapped), [arr(w.shape, f32) for w in weights],
            [scr(w.shape, f32) for w in weights] + [pltpu.SemaphoreType.DMA((3,))],
            [core, value.reshape(half.shape)] + list(grads), 10**7, "unpack", scalars=1, hbm=len(grads),
            far_outs=3, aliases={2 + index: index for index in range(len(grads))},
        )
    grad_zero, grad_one, grad_two = grads
    return updated[None], feature_grad[None], grad_zero, grad_one, grad_two


def solution(mesh):
    cores, rows, columns = SPLIT
    graph = mesh.shape["graph"]
    fine = jax.sharding.Mesh(mesh.devices.reshape(graph // cores, cores, rows, columns), ("z", "core", "x", "y"))
    dp, along = PLANE, ("z", "core")
    nodes, edges = P(dp, None, None, along), P(dp, along)
    in_specs = (nodes, nodes) + (P(),) * 4 + (edges,) * 4 + (P(dp, along, None),) * 5
    return jax.shard_map(
        body, mesh=fine, in_specs=in_specs, out_specs=(nodes, nodes, P(), P(), P()), check_vma=False
    )
```
